256 devices in a mesh: row: 64 (over z, y, core), col: 4 (over x).
Axes of the slice: x: 4, y: 4, z: 8, core: 2. Of those that a mesh axis runs over, the one named last changes fastest.
Arguments:
- design: bfloat16 [524288, 512], P('row', 'col'), may hold values from -6 to 6
- row_signs: int32 [524288], P('row'), may hold values from -1 to 1, as said below
- sampled: int32 [64, 256], P('row'), may hold values from 0 to 8191, as said below
Outputs:
- sketch: float32 [16384, 512], P('row', 'col')
- sketch_gram: float32 [512, 512], P('row', 'col')
The draws below stay inside these ranges and needn't reach their ends.
Inputs may be any that keep to these rules, and one draw needn't show every extreme that they name: `row_signs`: each entry is -1 or +1. `sampled`: each row is non-decreasing; offsets may repeat; in each row, entries s * 4 to (s + 1) * 4 - 1 lie in s * 128 to (s + 1) * 128 - 1, for every s below 64.
All inputs are finite; a program needn't handle non-finite values.
Results may differ from the reference program's by a relative error of at most 0.0003.
Values sent between devices are 32-bit elements; how exact they have to be, the bound alone decides.
A program may use at most 64 MiB of HBM per device.

```python
import jax
import jax.numpy as jnp
from jax import lax

C = 512
ROWS_DEV = 8192
SAMP_DEV = 256
ROWS = 524288
SAMPLES = 16384
N_ROW = 64


def draw_row_signs(key, part):
    key = jax.random.fold_in(key, 5)
    return (2 * jax.random.randint(key, (ROWS,), 0, 2) - 1).astype(jnp.int32)


def draw_sampled(key, part):
    key = jax.random.fold_in(key, 7)
    slice_len = ROWS_DEV // N_ROW
    group = SAMP_DEV // N_ROW
    offsets = jax.random.randint(key, (N_ROW, N_ROW, group), 0, slice_len)
    offsets = jnp.sort(offsets, axis=2)
    offsets = offsets + (jnp.arange(N_ROW, dtype=jnp.int32) * slice_len)[None, :, None]
    offsets = offsets.reshape(N_ROW, SAMP_DEV)
    offsets = offsets.at[:, 0].set(0)
    offsets = offsets.at[:, SAMP_DEV - 1].set(ROWS_DEV - 1)
    return offsets.astype(jnp.int32)


def level_of(stream_key, shape, shards, low, top_value):
    gain, own = 1.0, jax.random.fold_in(stream_key, 6)
    for position, blocks in shards:
        heights = jnp.exp(jax.random.uniform(jax.random.fold_in(own, position), (blocks,), jnp.float32, low / len(shards), top_value / len(shards)))
        gain = gain * jnp.repeat(heights, shape[position] // blocks).reshape([-1 if axis == position else 1 for axis in range(len(shape))])
    return gain


def noise(rng, dims, scale, reach, cuts=(), kind=jnp.bfloat16):
    gain = level_of(rng, dims, cuts, -0.22, 0.18) if cuts else 1.0
    array = jax.random.normal(rng, dims, jnp.float32) * scale * gain
    return jnp.minimum(jnp.maximum(array, -reach), reach).astype(kind)


def setup_inputs(seed: int = 0) -> dict:
    seeds = jax.random.split(jax.random.key(seed), 4)
    design = noise(seeds[0], (ROWS, C), 1.0, 6.0, ((0, 64), (1, 4)))
    row_signs = draw_row_signs(jax.random.fold_in(seeds[3], 71), 0)
    sampled = draw_sampled(jax.random.fold_in(seeds[3], 71), 0)
    return dict(design=design, row_signs=row_signs, sampled=sampled)


def hadamard(order):
    index = jnp.arange(order, dtype=jnp.int32)
    both = index[:, None] & index[None, :]
    parity = jnp.zeros((order, order), jnp.int32)
    for place in range(max(order.bit_length() - 1, 0)):
        parity = parity ^ ((both >> place) & 1)
    return (1 - 2 * parity).astype(jnp.float32)


def reference(design, row_signs, sampled):
    width = min(C, 128)
    outer = hadamard(N_ROW)
    middle = hadamard(ROWS_DEV // 128)
    inner = hadamard(128)
    scale = float(ROWS) ** -0.5
    picks = (jnp.arange(N_ROW, dtype=jnp.int32)[:, None] * ROWS_DEV + sampled).reshape(-1).astype(jnp.int32)
    blocks = design.reshape(ROWS, C // width, width).transpose(1, 0, 2)
    sign_col = row_signs.astype(jnp.float32)[:, None]

    def one_block(block):
        field = block.astype(jnp.float32) * sign_col
        field = field.reshape(N_ROW, ROWS_DEV // 128, 128, width)
        field = jnp.einsum("ab,dbjc->dajc", middle, field, precision=lax.Precision.HIGHEST)
        field = jnp.einsum("ij,dajc->daic", inner, field, precision=lax.Precision.HIGHEST)
        field = jnp.einsum("ed,dajc->eajc", outer, field, precision=lax.Precision.HIGHEST)
        field = field.reshape(ROWS, width) * scale
        return field[picks]

    picked = lax.map(one_block, blocks)
    sketch = picked.transpose(1, 0, 2).reshape(SAMPLES, C)
    gram = jnp.dot(sketch.T, sketch, precision=lax.Precision.HIGHEST, preferred_element_type=jnp.float32) / SAMPLES
    return sketch, gram
```

```python
import functools

import jax
import jax.numpy as jnp
from jax import lax
from jax.experimental import pallas as pl
from jax.experimental.pallas import tpu as pltpu
from jax.sharding import PartitionSpec as P

MESH = pl.DeviceIdType.MESH
NZ, NY = 8, 4
F32, BF16 = jnp.float32, jnp.bfloat16
CHUNKS = 4
PAIRS = 16
PARTS = (("z", 0, 4), ("y", 0, 4), ("z", 1, 4), ("y", 1, 4))


def split(v):
    high = v.astype(BF16)
    return high, (v - high.astype(F32)).astype(BF16)


def parity_sign(v):
    return (1 - 2 * (((v >> 2) ^ (v >> 1) ^ v) & 1)).astype(F32)


class Part:
    def __init__(self, kind, refs):
        self.axis, self.longer, self.pairs = kind
        self.q, self.r1, self.f, self.r2, self.s1, self.v1, self.s2, self.v2 = refs


class Arm:
    def __init__(self, me, n, step, reach, own, recv, slot, send_sem, recv_sem, device, sent):
        self.me, self.n, self.step, self.reach, self.own = me, n, step, reach, own
        self.recv, self.slot, self.sent = recv, slot, sent
        self.send_sem, self.recv_sem = send_sem, recv_sem
        self.device = device(self.at(step))
        self.copies = {}

    def at(self, offset):
        return lax.rem(self.me + self.n + offset, self.n)

    def start(self, s):
        if not 1 <= s <= self.reach:
            return
        index = self.slot + s - 1
        source = self.own(self.at(self.step * self.reach)) if s == 1 else self.recv.at[index - 1]
        copy = pltpu.make_async_remote_copy(
            src_ref=source,
            dst_ref=self.recv.at[index],
            send_sem=self.send_sem.at[index],
            recv_sem=self.recv_sem.at[index],
            device_id=self.device,
            device_id_type=MESH,
        )
        copy.start()
        self.copies[s] = copy
        self.sent.append(copy)

    def take(self, s):
        if not 1 <= s <= self.reach:
            return
        self.copies[s].wait_recv()
        if s < self.reach:
            here = self.recv.at[self.slot + s - 1]
            here[...] = here[...] + self.own(self.at(self.step * (self.reach - s)))[...]
            self.start(s + 1)


def kernel(
    nx, x_hbm, sgn_ref, smp_ref, sk_out, g_out,
    x_v, own, out_t, in_t, sloc, sidx, signs, sk, sib, xg, gbuf, g1, g1s, g2,
    load_sem, t_send, t_recv, i_send, i_recv, j_send, j_recv, x_send, x_recv, o_send, o_recv,
    g_send, g_recv, h_send, h_recv, *part_refs,
):
    row, col = lax.axis_index("row"), lax.axis_index("col")
    c = lax.rem(row, 2)
    yc = lax.rem(row, 2 * NY)
    y = yc // 2
    z = row // (2 * NY)
    nyc = 2 * NY
    half = PAIRS * 2
    sent = []

    def at_yc(v):
        return (z * nyc + v, col)

    def at_z(v):
        return (v * nyc + yc, col)

    def at_y(v):
        return (z * nyc + v * 2 + c, col)

    sibling = (row + 1 - 2 * c, col)

    barrier = pltpu.get_barrier_semaphore()
    for k in range(1, nyc):
        pl.semaphore_signal(barrier, inc=1, device_id=at_yc(lax.rem(yc + k, nyc)), device_id_type=MESH)
    for k in range(1, NZ):
        pl.semaphore_signal(barrier, inc=1, device_id=at_z(lax.rem(z + k, NZ)), device_id_type=MESH)
    for k in range(1, nx):
        pl.semaphore_signal(barrier, inc=1, device_id=(row, lax.rem(col + k, nx)), device_id_type=MESH)

    step = half // CHUNKS
    loads = []
    for g in range(CHUNKS):
        for top in range(2):
            rows = pl.ds(top * half + g * step, step)
            load = pltpu.make_async_copy(x_hbm.at[rows], x_v.at[rows], load_sem.at[2 * g + top])
            load.start()
            loads.append(load)

    for h in range(2):
        sloc[h] = smp_ref[:, h * 128 : (h + 1) * 128] & 127
    sidx[z, pl.ds(yc, 1), :] = sloc[c]

    pl.semaphore_wait(barrier, nyc - 1 + NZ - 1 + nx - 1)

    to_plane = []
    for k in range(1, nyc):
        there = lax.rem(yc + k, nyc)
        copy = pltpu.make_async_remote_copy(
            src_ref=sloc.at[lax.rem(there, 2)],
            dst_ref=sidx.at[z, pl.ds(yc, 1), :],
            send_sem=i_send.at[k - 1],
            recv_sem=i_recv.at[k - 1],
            device_id=at_yc(there),
            device_id_type=MESH,
        )
        copy.start()
        to_plane.append(copy)
    sent += to_plane

    lane = lax.broadcasted_iota(jnp.int32, (128, 128), 1)
    eye = (lane == lax.broadcasted_iota(jnp.int32, (128, 128), 0)).astype(F32)
    flip = (1 - 2 * c).astype(F32)
    t_copies = []
    for g in range(CHUNKS):
        loads[2 * g].wait()
        loads[2 * g + 1].wait()

        def first(i, _):
            a = g * step + i
            d0 = (eye * sgn_ref[pl.ds(a, 1), :].astype(F32)).astype(BF16)
            d1 = (eye * (sgn_ref[pl.ds(half + a, 1), :].astype(F32) * flip)).astype(BF16)
            v0 = jnp.dot(d0, x_v[a], preferred_element_type=F32)
            v1 = jnp.dot(d1, x_v[half + a], preferred_element_type=F32)
            out_t[a] = v0 - v1
            own[a] = v0 + v1
            return 0

        lax.fori_loop(0, step, first, 0, unroll=4)
        rows = pl.ds(g * step, step)
        copy = pltpu.make_async_remote_copy(
            src_ref=out_t.at[rows],
            dst_ref=in_t.at[rows],
            send_sem=t_send.at[g],
            recv_sem=t_recv.at[g],
            device_id=sibling,
            device_id_type=MESH,
        )
        copy.start()
        t_copies.append(copy)
    sent += t_copies

    for copy in to_plane:
        copy.wait_recv()
    along_z = []
    for k in range(1, NZ):
        copy = pltpu.make_async_remote_copy(
            src_ref=sidx.at[z],
            dst_ref=sidx.at[z],
            send_sem=j_send.at[k - 1],
            recv_sem=j_recv.at[k - 1],
            device_id=at_z(lax.rem(z + k, NZ)),
            device_id_type=MESH,
        )
        copy.start()
        along_z.append(copy)
    sent += along_z

    def transform(ref):
        def body(i, _):
            rows = pl.ds(pl.multiple_of(i * 8, 8), 8)
            v = [ref[a, rows, :] for a in range(half)]
            place = 1
            while place < half:
                for a in range(half):
                    if not a & place:
                        v[a], v[a | place] = v[a] + v[a | place], v[a] - v[a | place]
                place *= 2
            for a in range(half):
                ref[a, rows, :] = v[a]
            return 0

        lax.fori_loop(0, 16, body, 0)

    transform(own)

    for copy in along_z:
        copy.wait_recv()
    nb = NZ * nyc
    table = sidx[...].reshape(nb, 128).astype(F32)
    if nb < 128:
        table = jnp.concatenate([table, jnp.zeros((128 - nb, 128), F32)], axis=0)
    table = table.T.astype(jnp.int32)
    for bz in range(NZ):
        for by in range(NY):
            chip = parity_sign(bz & z) * parity_sign(by & y)
            rows = []
            for bc in range(2):
                b = bz * nyc + by * 2 + bc
                index = jnp.broadcast_to(table[:, b : b + 1], (128, 128))
                odd = (lax.population_count(index & lane) & 1).astype(F32)
                gain = chip * flip if bc else chip
                rows.append((gain - (2 * gain) * odd).reshape(PAIRS, 8, 128))
            mine = jnp.concatenate(rows, axis=1).astype(BF16)
            theirs = jnp.concatenate([rows[0], -rows[1]], axis=1).astype(BF16)
            first_pair = 0
            for axis, _, pairs in PARTS:
                place = bz * NY + by if axis == "z" else by * NZ + bz
                here = slice(first_pair, first_pair + pairs)
                signs[here, place * 16 : place * 16 + 16, :128] = mine[here]
                signs[here, place * 16 : place * 16 + 16, 128:] = theirs[here]
                first_pair += pairs

    for copy in t_copies:
        copy.wait_recv()
    transform(in_t)

    chips = NZ * NY
    lower = lax.broadcasted_iota(jnp.int32, (chips * 16, 128), 0) % 8 < 4
    parts, arms = [], []
    first_pair = 0
    for number, kind in enumerate(PARTS):
        part = Part(kind, part_refs[8 * number : 8 * number + 8])
        parts.append(part)
        n1, n2 = (NZ, NY) if part.axis == "z" else (NY, NZ)

        def product(i, _):
            p = first_pair + i
            field = jnp.concatenate(
                [
                    jnp.concatenate([own[2 * p], own[2 * p + 1]], axis=1),
                    jnp.concatenate([in_t[2 * p], in_t[2 * p + 1]], axis=1),
                ],
                axis=0,
            )
            high, low = split(field)
            both = jnp.dot(signs[p], high, preferred_element_type=F32) + jnp.dot(
                signs[p], low, preferred_element_type=F32
            )
            value = jnp.where(lower, both[:, :128], both[:, 128:])
            part.q[:, :, i] = value.reshape(n1, n2, 2, 8, 128)
            return 0

        lax.fori_loop(0, part.pairs, product, 0)
        first_pair += part.pairs
        me, device = (z, at_z) if part.axis == "z" else (y, at_y)
        long, short = n1 // 2, n1 - 1 - n1 // 2
        up, down = (short, long) if part.longer else (long, short)
        own_block = functools.partial(lambda q, t: q.at[t], part.q)
        args = (own_block, part.r1)
        part.up = Arm(me, n1, 1, up, *args, 0, part.s1, part.v1, device, sent)
        part.down = Arm(me, n1, -1, down, *args, up, part.s1, part.v1, device, sent)
        part.reach = long
        part.up.start(1)
        part.down.start(1)

    def turn(part):
        part.up.take(part.up.reach)
        part.down.take(part.down.reach)
        total = part.q[part.up.me]
        if part.up.reach:
            total = total + part.r1[part.up.slot + part.up.reach - 1]
        if part.down.reach:
            total = total + part.r1[part.down.slot + part.down.reach - 1]
        part.f[...] = total
        n2 = NY if part.axis == "z" else NZ
        me, device = (y, at_y) if part.axis == "z" else (z, at_z)
        long, short = n2 // 2, n2 - 1 - n2 // 2
        up, down = (short, long) if part.longer else (long, short)
        own_block = functools.partial(lambda f, t: f.at[t], part.f)
        args = (own_block, part.r2)
        part.up2 = Arm(me, n2, 1, up, *args, 0, part.s2, part.v2, device, sent)
        part.down2 = Arm(me, n2, -1, down, *args, up, part.s2, part.v2, device, sent)
        part.reach2 = long
        part.up2.start(1)
        part.down2.start(1)

    scale = float(8192 * NZ * nyc) ** (-0.5)
    x_copies = []

    def finish(part, number):
        part.up2.take(part.up2.reach)
        part.down2.take(part.down2.reach)
        total = part.f[part.up2.me]
        if part.up2.reach:
            total = total + part.r2[part.up2.slot + part.up2.reach - 1]
        if part.down2.reach:
            total = total + part.r2[part.down2.slot + part.down2.reach - 1]
        first = sum(kind[2] for kind in PARTS[:number])
        here = pl.ds(first, part.pairs)
        sk[:, here] = jnp.swapaxes(total * scale, 0, 1)
        for k in range(1, nx):
            copy = pltpu.make_async_remote_copy(
                src_ref=sk.at[:, here],
                dst_ref=xg.at[k - 1, :, here],
                send_sem=x_send.at[k - 1, number],
                recv_sem=x_recv.at[k - 1, number],
                device_id=(row, lax.rem(col + k, nx)),
                device_id_type=MESH,
            )
            copy.start()
            x_copies.append((k, copy))
            sent.append(copy)

    def advance(part, s):
        if s < part.up.reach:
            part.up.take(s)
        if s < part.down.reach:
            part.down.take(s)

    def advance2(part, s):
        if s < part.up2.reach:
            part.up2.take(s)
        if s < part.down2.reach:
            part.down2.take(s)

    z_parts = [p for p in parts if p.axis == "z"]
    y_parts = [p for p in parts if p.axis == "y"]
    for s in range(1, NZ // 2):
        for part in z_parts:
            advance(part, s)
        for part in y_parts:
            advance(part, s)
    for part in y_parts:
        turn(part)
    for part in z_parts:
        turn(part)
    for s in range(1, NZ // 2):
        for part in y_parts:
            advance2(part, s)
        for part in z_parts:
            advance2(part, s)
    for part in z_parts + y_parts:
        finish(part, parts.index(part))

    swap = pltpu.make_async_remote_copy(
        src_ref=sk.at[1 - c],
        dst_ref=sib,
        send_sem=o_send.at[0],
        recv_sem=o_recv.at[0],
        device_id=sibling,
        device_id_type=MESH,
    )
    swap.start()
    sent.append(swap)
    sk_out[c] = sk[c]

    gr = nx * 128 // nb
    per_x = NZ // nx
    mine_high, mine_low = split(sk[...].reshape(256, 128))
    for k in range(nx):
        if k:
            for which, copy in x_copies:
                if which == k:
                    copy.wait_recv()
            high, low = split(xg[k - 1].reshape(256, 128))
        else:
            high, low = mine_high, mine_low
        dims = (((0,), (0,)), ((), ()))
        block = (
            lax.dot_general(high, mine_high, dims, preferred_element_type=F32)
            + lax.dot_general(high, mine_low, dims, preferred_element_type=F32)
            + lax.dot_general(low, mine_high, dims, preferred_element_type=F32)
        ).reshape(per_x, nyc, gr, 128)
        from_x = lax.rem(col + nx - k, nx)
        for i in range(per_x):
            gbuf[:, from_x * per_x + i] = block[i]

    in_plane = []
    for k in range(1, nyc):
        there = lax.rem(yc + k, nyc)
        copy = pltpu.make_async_remote_copy(
            src_ref=gbuf.at[there],
            dst_ref=g1.at[k - 1],
            send_sem=g_send.at[k - 1],
            recv_sem=g_recv.at[k - 1],
            device_id=at_yc(there),
            device_id_type=MESH,
        )
        copy.start()
        in_plane.append(copy)
    sent += in_plane
    total = gbuf[yc]
    for k, copy in enumerate(in_plane):
        copy.wait_recv()
        total = total + g1[k]
    g1s[...] = total
    in_column = []
    for k in range(1, NZ):
        there = lax.rem(z + k, NZ)
        copy = pltpu.make_async_remote_copy(
            src_ref=g1s.at[there],
            dst_ref=g2.at[k - 1],
            send_sem=h_send.at[k - 1],
            recv_sem=h_recv.at[k - 1],
            device_id=at_z(there),
            device_id_type=MESH,
        )
        copy.start()
        in_column.append(copy)
    sent += in_column
    swap.wait_recv()
    sk_out[1 - c] = sib[...]
    total = g1s[z]
    for k, copy in enumerate(in_column):
        copy.wait_recv()
        total = total + g2[k]
    g_out[...] = total * (1.0 / float(256 * nb))
    for copy in sent:
        copy.wait_send()


def on_device(nx, design, row_signs, sampled):
    vm, dma = pltpu.VMEM, pltpu.SemaphoreType.DMA
    half = PAIRS * 2
    nyc = 2 * NY
    nb = NZ * nyc
    gr = nx * 128 // nb
    scratch = [
        vm((2 * half, 128, 128), BF16),
        vm((half, 128, 128), F32),
        vm((half, 128, 128), F32),
        vm((half, 128, 128), F32),
        vm((2, 1, 128), jnp.int32),
        vm((NZ, nyc, 128), jnp.int32),
        vm((PAIRS, NZ * NY * 16, 256), BF16),
        vm((2, PAIRS, 8, 128), F32),
        vm((PAIRS, 8, 128), F32),
        vm((max(nx - 1, 1), 2, PAIRS, 8, 128), F32),
        vm((nyc, NZ, gr, 128), F32),
        vm((nyc - 1, NZ, gr, 128), F32),
        vm((NZ, gr, 128), F32),
        vm((NZ - 1, gr, 128), F32),
        dma((2 * CHUNKS,)),
        dma((CHUNKS,)),
        dma((CHUNKS,)),
        dma((nyc - 1,)),
        dma((nyc - 1,)),
        dma((NZ - 1,)),
        dma((NZ - 1,)),
        dma((max(nx - 1, 1), len(PARTS))),
        dma((max(nx - 1, 1), len(PARTS))),
        dma((1,)),
        dma((1,)),
        dma((nyc - 1,)),
        dma((nyc - 1,)),
        dma((NZ - 1,)),
        dma((NZ - 1,)),
    ]
    for axis, _, pairs in PARTS:
        n1, n2 = (NZ, NY) if axis == "z" else (NY, NZ)
        scratch += [
            vm((n1, n2, pairs, 2, 8, 128), F32),
            vm((n1 - 1, n2, pairs, 2, 8, 128), F32),
            vm((n2, pairs, 2, 8, 128), F32),
            vm((n2 - 1, pairs, 2, 8, 128), F32),
            dma((n1 - 1,)),
            dma((n1 - 1,)),
            dma((n2 - 1,)),
            dma((n2 - 1,)),
        ]
    sketch, gram = pl.pallas_call(
        functools.partial(kernel, nx),
        out_shape=(
            jax.ShapeDtypeStruct((2, PAIRS, 8, 128), F32),
            jax.ShapeDtypeStruct((gr, 128), F32),
        ),
        in_specs=[
            pl.BlockSpec(memory_space=pl.ANY),
            pl.BlockSpec(memory_space=pltpu.VMEM),
            pl.BlockSpec(memory_space=pltpu.VMEM),
        ],
        out_specs=(pl.BlockSpec(memory_space=pltpu.VMEM), pl.BlockSpec(memory_space=pltpu.VMEM)),
        scratch_shapes=scratch,
        compiler_params=pltpu.CompilerParams(
            collective_id=0, has_side_effects=True, vmem_limit_bytes=48 * 1024 * 1024
        ),
    )(design.reshape(2 * half, 128, 128), row_signs.reshape(2 * half, 128), sampled)
    return sketch.reshape(256, 128), gram


def solution(mesh):
    return jax.shard_map(
        functools.partial(on_device, mesh.shape["col"]),
        mesh=mesh,
        in_specs=(P("row", "col"), P("row"), P("row", None)),
        out_specs=(P("row", "col"), P("row", "col")),
        check_vma=False,
    )
```

```python
import functools

import jax
import jax.numpy as jnp
from jax import lax
from jax.experimental import pallas as pl
from jax.experimental.pallas import tpu as pltpu
from jax.sharding import PartitionSpec as P

MESH = pl.DeviceIdType.MESH
NZ, NY = 8, 4
F32, BF16 = jnp.float32, jnp.bfloat16
CHUNKS = 4
PAIRS = 16
PARTS = (
    ("z", 2, 0, True),
    ("y", 2, 0, False),
    ("z", 2, 1, True),
    ("y", 2, 1, False),
    ("z", 2, 0, True),
    ("y", 2, 0, False),
    ("z", 2, 1, True),
    ("y", 2, 1, False),
)
ORDER = (
    (0, 1, 0, 1), (0, 1, 1, 1), (2, 1, 0, 1), (2, 1, 1, 1), (1, 1, 0, 1), (1, 1, 1, 1), (4, 1, 0, 1), (4, 1, 1, 1),
    (0, 1, 0, 2), (3, 1, 0, 1), (3, 1, 1, 1), (0, 1, 1, 2), (6, 1, 0, 1), (6, 1, 1, 1), (2, 1, 0, 2), (5, 1, 0, 1),
    (5, 1, 1, 1), (2, 1, 1, 2), (4, 1, 0, 2), (4, 1, 1, 2), (0, 1, 0, 3), (7, 1, 0, 1), (7, 1, 1, 1), (0, 1, 1, 3),
    (6, 1, 0, 2), (6, 1, 1, 2), (2, 1, 0, 3), (1, 1, 0, 2), (3, 1, 1, 2), (2, 1, 1, 3), (4, 1, 0, 3), (4, 1, 1, 3),
    (0, 1, 0, 4), (5, 1, 0, 2), (7, 1, 1, 2), (6, 1, 1, 3), (1, 2, 1, 1), (3, 2, 1, 1), (6, 1, 0, 3), (1, 2, 0, 1),
    (3, 2, 0, 1), (2, 1, 1, 4), (5, 2, 1, 1), (7, 2, 1, 1), (4, 1, 0, 4), (5, 2, 0, 1), (0, 2, 0, 1), (7, 2, 0, 1),
    (1, 2, 0, 2), (6, 1, 1, 4), (3, 2, 0, 2), (1, 2, 1, 2), (3, 2, 1, 2), (5, 2, 1, 2), (2, 2, 0, 1), (7, 2, 1, 2),
    (5, 2, 0, 2), (7, 2, 0, 2), (4, 2, 0, 1), (1, 2, 0, 3), (3, 2, 0, 3), (1, 2, 1, 3), (3, 2, 1, 3), (6, 2, 0, 1),
    (5, 2, 1, 3), (7, 2, 1, 3), (5, 2, 0, 3), (7, 2, 0, 3), (1, 2, 0, 4), (3, 2, 1, 4), (7, 2, 1, 4), (5, 2, 0, 4),
)


def split(v):
    high = v.astype(BF16)
    return high, (v - high.astype(F32)).astype(BF16)


class Arm:
    def __init__(self, me, n, step, reach, own, recv, slot, send_sem, recv_sem, device, sent):
        self.me, self.n, self.step, self.reach, self.own = me, n, step, reach, own
        self.recv, self.slot, self.sent = recv, slot, sent
        self.send_sem, self.recv_sem = send_sem, recv_sem
        self.device = device(self.at(step))
        self.copies = {}

    def at(self, offset):
        return lax.rem(self.me + self.n + offset, self.n)

    def start(self, s):
        if not 1 <= s <= self.reach:
            return
        index = self.slot + s - 1
        source = self.own(self.at(self.step * self.reach)) if s == 1 else self.recv.at[index - 1]
        copy = pltpu.make_async_remote_copy(
            src_ref=source,
            dst_ref=self.recv.at[index],
            send_sem=self.send_sem.at[index],
            recv_sem=self.recv_sem.at[index],
            device_id=self.device,
            device_id_type=MESH,
        )
        copy.start()
        self.copies[s] = copy
        self.sent.append(copy)

    def take(self, s):
        self.copies[s].wait_recv()
        if s < self.reach:
            here = self.recv.at[self.slot + s - 1]
            here[...] = here[...] + self.own(self.at(self.step * (self.reach - s)))[...]
            self.start(s + 1)


class Stage:
    def __init__(self, me, n, longer, direct, source, recv, send_sem, recv_sem, device, sent):
        self.me, self.source, self.recv = me, source, recv
        self.direct = []
        self.arms = []
        if direct:
            for k in range(1, n):
                there = lax.rem(me + k, n)
                copy = pltpu.make_async_remote_copy(
                    src_ref=source.at[there],
                    dst_ref=recv.at[k - 1],
                    send_sem=send_sem.at[k - 1],
                    recv_sem=recv_sem.at[k - 1],
                    device_id=device(there),
                    device_id_type=MESH,
                )
                copy.start()
                sent.append(copy)
                self.direct.append(copy)
            self.left = 1
            self.last = list(range(n - 1))
            return
        long, short = n // 2, n - 1 - n // 2
        up, down = (short, long) if longer else (long, short)
        own = lambda t: source.at[t]
        for step, reach, slot in ((1, up, 0), (-1, down, up)):
            self.arms.append(Arm(me, n, step, reach, own, recv, slot, send_sem, recv_sem, device, sent))
            self.arms[-1].start(1)
        self.left = n - 1
        self.last = [arm.slot + arm.reach - 1 for arm in self.arms if arm.reach]

    def take(self, direction, step):
        if self.direct:
            for copy in self.direct:
                copy.wait_recv()
        elif step <= self.arms[direction].reach:
            self.arms[direction].take(step)
        else:
            return False
        self.left -= 1
        return self.left == 0

    def total(self):
        value = self.source[self.me]
        for slot in self.last:
            value = value + self.recv[slot]
        return value


def kernel(
    nx, x_hbm, sgn_hbm, smp_hbm, sk_out, g_out,
    x_v, sgn_ref, smp_ref, own, out_t, in_t, sloc, sidx, table, signs0, signs1, sk, xg, gbuf, g2,
    load_sem, t_send, t_recv, i_send, i_recv, x_send, x_recv, h_send, h_recv, *part_refs,
):
    row, col = lax.axis_index("row"), lax.axis_index("col")
    c = lax.rem(row, 2)
    chip = row // 2
    y = lax.rem(chip, NY)
    z = chip // NY
    chips = NZ * NY
    half = PAIRS * 2
    sent = []

    rows_all = 2 * chips
    other = 1 - c

    def at_chip(v):
        return (v * 2 + c, col)

    def at_z(v):
        return at_chip(v * NY + y)

    def at_y(v):
        return at_chip(z * NY + v)

    def other_chip(k):
        return lax.rem(chip + k, chips)

    def other_row(k):
        return lax.rem(row + k, rows_all)

    def other_col(k):
        return lax.rem(col + k, nx)

    beside = row + 1 - 2 * c
    sibling = (beside, col)

    small = []
    for number, (source, target) in enumerate(((smp_hbm, smp_ref), (sgn_hbm, sgn_ref))):
        load = pltpu.make_async_copy(source, target, load_sem.at[2 * CHUNKS + number])
        load.start()
        small.append(load)
    step = half // CHUNKS
    loads = []
    for g in range(CHUNKS):
        for top in range(2):
            rows = pl.ds(top * half + g * step, step)
            load = pltpu.make_async_copy(x_hbm.at[rows], x_v.at[rows], load_sem.at[2 * g + top])
            load.start()
            loads.append(load)

    barrier = pltpu.get_barrier_semaphore()
    for k in range(1, rows_all):
        pl.semaphore_signal(barrier, inc=1, device_id=(other_row(k), col), device_id_type=MESH)
    for k in range(1, nx):
        for there in (row, beside):
            pl.semaphore_signal(barrier, inc=1, device_id=(there, other_col(k)), device_id_type=MESH)

    small[0].wait()
    for h in range(2):
        sloc[h] = smp_ref[:, h * 128 : (h + 1) * 128] & 127
    sidx[z, pl.ds(2 * y + c, 1), :] = sloc[c]
    small[1].wait()

    lane = lax.broadcasted_iota(jnp.int32, (128, 128), 1)
    eye = (lane == lax.broadcasted_iota(jnp.int32, (128, 128), 0)).astype(F32)
    flip = (1 - 2 * c).astype(F32)
    t_copies = []
    for g in range(CHUNKS):
        loads[2 * g].wait()
        loads[2 * g + 1].wait()

        def first(i, _):
            a = g * step + i
            d0 = (eye * sgn_ref[pl.ds(a, 1), :].astype(F32)).astype(BF16)
            d1 = (eye * (sgn_ref[pl.ds(half + a, 1), :].astype(F32) * flip)).astype(BF16)
            v0 = jnp.dot(d0, x_v[a], preferred_element_type=F32)
            v1 = jnp.dot(d1, x_v[half + a], preferred_element_type=F32)
            out_t[a] = v0 - v1
            own[a] = v0 + v1
            return 0

        lax.fori_loop(0, step, first, 0, unroll=4)
        if g == 0:
            pl.semaphore_wait(barrier, rows_all - 1 + 2 * (nx - 1))
        rows = pl.ds(g * step, step)
        copy = pltpu.make_async_remote_copy(
            src_ref=out_t.at[rows],
            dst_ref=in_t.at[rows],
            send_sem=t_send.at[g],
            recv_sem=t_recv.at[g],
            device_id=sibling,
            device_id_type=MESH,
        )
        copy.start()
        t_copies.append(copy)
        if g == 0:
            to_rows = []
            for k in range(1, rows_all):
                copy = pltpu.make_async_remote_copy(
                    src_ref=sloc.at[lax.rem(row + k, 2)],
                    dst_ref=sidx.at[z, pl.ds(2 * y + c, 1), :],
                    send_sem=i_send.at[k - 1],
                    recv_sem=i_recv.at[k - 1],
                    device_id=(other_row(k), col),
                    device_id_type=MESH,
                )
                copy.start()
                to_rows.append(copy)
            sent += to_rows
    sent += t_copies

    def transform(ref):
        def body(i, _):
            rows = pl.ds(pl.multiple_of(i * 8, 8), 8)
            v = [ref[a, rows, :] for a in range(half)]
            place = 1
            while place < half:
                for a in range(half):
                    if not a & place:
                        v[a], v[a | place] = v[a] + v[a | place], v[a] - v[a | place]
                place *= 2
            for a in range(half):
                ref[a, rows, :] = v[a]
            return 0

        lax.fori_loop(0, 16, body, 0)

    transform(own)

    for copy in to_rows:
        copy.wait_recv()
    nb = rows_all
    index = sidx[...].reshape(nb, 128).astype(F32)
    if nb < 128:
        index = jnp.concatenate([index, jnp.zeros((128 - nb, 128), F32)], axis=0)
    negative = lax.population_count(lane & row) & 1
    table[...] = (index.T.astype(jnp.int32) + 128 * negative).reshape(PAIRS, 8, 128)

    for copy in t_copies:
        copy.wait_recv()
    transform(in_t)

    lower = lax.broadcasted_iota(jnp.int32, (chips * 16, 128), 0) % 8 < 4
    place8 = lax.broadcasted_iota(jnp.int32, (8, 128), 1) + 128
    axes = {"z": (z, NZ, at_z), "y": (y, NY, at_y)}
    stages = {}
    firsts = [sum(kind[1] for kind in PARTS[:number]) for number in range(len(PARTS))]
    for number, (axis, pairs, longer, direct) in enumerate(PARTS):
        q, r1, f, r2, s1, v1, s2, v2 = part_refs[8 * number : 8 * number + 8]
        first_pair = firsts[number]
        n1, n2 = (NZ, NY) if axis == "z" else (NY, NZ)

        def one(p, i, signs):
            index = table[p]
            for place in range(chips):
                bz, by = (place // NY, place % NY) if axis == "z" else (place % NZ, place // NZ)
                rows = []
                for bc in range(2):
                    b = (bz * NY + by) * 2 + bc
                    ours = jnp.broadcast_to(index[:, b : b + 1], (8, 128)) & place8
                    rows.append((1 - 2 * (lax.population_count(ours) & 1)).astype(F32))
                here = pl.ds(place * 16, 16)
                signs[here, :128] = jnp.concatenate(rows, axis=0).astype(BF16)
                signs[here, 128:] = jnp.concatenate([rows[0], -rows[1]], axis=0).astype(BF16)
            field = jnp.concatenate(
                [
                    jnp.concatenate([own[2 * p], own[2 * p + 1]], axis=1),
                    jnp.concatenate([in_t[2 * p], in_t[2 * p + 1]], axis=1),
                ],
                axis=0,
            )
            high, low = split(field)
            both = jnp.dot(signs[...], high, preferred_element_type=F32) + jnp.dot(
                signs[...], low, preferred_element_type=F32
            )
            value = jnp.where(lower, both[:, :128], both[:, 128:])
            q[:, :, i] = value.reshape(n1, n2, 2, 8, 128)

        def product(i, _):
            one(first_pair + 2 * i, 2 * i, signs0)
            one(first_pair + 2 * i + 1, 2 * i + 1, signs1)
            return 0

        if pairs > 1:
            lax.fori_loop(0, pairs // 2, product, 0)
        if pairs % 2:
            one(first_pair + pairs - 1, pairs - 1, signs0)
        me, n, device = axes[axis]
        stages[number, 1] = Stage(me, n, longer, False, q, r1, s1, v1, device, sent)

    scale = float(8192 * nb) ** (-0.5)
    x_copies = []

    def finish(number):
        here = pl.ds(firsts[number], PARTS[number][1])
        sk[:, here] = jnp.swapaxes(stages[number, 2].total() * scale, 0, 1)
        for k in range(nx):
            for slot, there in enumerate((row, beside)):
                if k or slot:
                    copy = pltpu.make_async_remote_copy(
                        src_ref=sk.at[:, here],
                        dst_ref=xg.at[k, slot, :, here],
                        send_sem=x_send.at[k, slot, number],
                        recv_sem=x_recv.at[k, slot, number],
                        device_id=(there, other_col(k)),
                        device_id_type=MESH,
                    )
                    copy.start()
                    x_copies.append((number, copy))
                    sent.append(copy)

    gr = nx * 128 // nb
    per_x = chips // nx
    dims = (((0,), (0,)), ((), ()))

    def rows_of(ref, numbers):
        pieces = []
        for number in numbers:
            pieces.append(ref[:, firsts[number] : firsts[number] + PARTS[number][1]].reshape(-1, 128))
        return pieces

    def gram(numbers, begin):
        for number, copy in x_copies:
            if number in numbers:
                copy.wait_recv()
        near = split(jnp.concatenate(rows_of(sk, numbers) + rows_of(xg.at[0, 1], numbers), axis=0))
        for k in range(nx):
            if k:
                far = split(jnp.concatenate(rows_of(xg.at[k, 0], numbers) + rows_of(xg.at[k, 1], numbers), axis=0))
            else:
                far = near
            block = (
                lax.dot_general(far[0], near[0], dims, preferred_element_type=F32)
                + lax.dot_general(far[0], near[1], dims, preferred_element_type=F32)
                + lax.dot_general(far[1], near[0], dims, preferred_element_type=F32)
            ).reshape(per_x, 2, gr, 128)
            here = pl.ds(lax.rem(col + nx - k, nx) * per_x, per_x)
            for core in range(2):
                value = block[:, core]
                gbuf[core, here] = value if begin else gbuf[core, here] + value

    done = []
    for number, phase, direction, step in ORDER:
        if not stages[number, phase].take(direction, step):
            continue
        if phase == 2:
            finish(number)
            done.append(number)
            continue
        axis, pairs, longer, direct = PARTS[number]
        q, r1, f, r2, s1, v1, s2, v2 = part_refs[8 * number : 8 * number + 8]
        f[...] = stages[number, 1].total()
        me, n, device = axes["y" if axis == "z" else "z"]
        stages[number, 2] = Stage(me, n, longer, direct, f, r2, s2, v2, device, sent)
    gram(done[: len(done) // 2], True)
    gram(done[len(done) // 2 :], False)

    blocks = []
    for k in range(1, chips):
        there = other_chip(k)
        copy = pltpu.make_async_remote_copy(
            src_ref=gbuf.at[c, there],
            dst_ref=g2.at[k - 1],
            send_sem=h_send.at[k - 1],
            recv_sem=h_recv.at[k - 1],
            device_id=at_chip(there),
            device_id_type=MESH,
        )
        copy.start()
        blocks.append(copy)
    sk_out[c] = sk[c]
    sk_out[other] = xg[0, 1, c]
    for copy in sent:
        copy.wait_send()
    total = gbuf[c, chip]
    for k, copy in enumerate(blocks):
        copy.wait_recv()
        total = total + g2[k]
    g_out[...] = total * (1.0 / float(256 * nb))
    for copy in blocks:
        copy.wait_send()


def on_device(nx, design, row_signs, sampled):
    vm, dma = pltpu.VMEM, pltpu.SemaphoreType.DMA
    half = PAIRS * 2
    chips = NZ * NY
    gr = nx * 128 // (2 * chips)
    scratch = [
        vm((2 * half, 128, 128), BF16),
        vm((2 * half, 128), jnp.int32),
        vm((1, 256), jnp.int32),
        vm((half, 128, 128), F32),
        vm((half, 128, 128), F32),
        vm((half, 128, 128), F32),
        vm((2, 1, 128), jnp.int32),
        vm((NZ, 2 * NY, 128), jnp.int32),
        vm((PAIRS, 8, 128), jnp.int32),
        vm((chips * 16, 256), BF16),
        vm((chips * 16, 256), BF16),
        vm((2, PAIRS, 8, 128), F32),
        vm((nx, 2, 2, PAIRS, 8, 128), F32),
        vm((2, chips, gr, 128), F32),
        vm((chips - 1, gr, 128), F32),
        dma((2 * CHUNKS + 2,)),
        dma((CHUNKS,)),
        dma((CHUNKS,)),
        dma((2 * chips - 1,)),
        dma((2 * chips - 1,)),
        dma((nx, 2, len(PARTS))),
        dma((nx, 2, len(PARTS))),
        dma((chips - 1,)),
        dma((chips - 1,)),
    ]
    for axis, pairs, _, _ in PARTS:
        n1, n2 = (NZ, NY) if axis == "z" else (NY, NZ)
        scratch += [
            vm((n1, n2, pairs, 2, 8, 128), F32),
            vm((n1 - 1, n2, pairs, 2, 8, 128), F32),
            vm((n2, pairs, 2, 8, 128), F32),
            vm((n2 - 1, pairs, 2, 8, 128), F32),
            dma((n1 - 1,)),
            dma((n1 - 1,)),
            dma((n2 - 1,)),
            dma((n2 - 1,)),
        ]
    sketch, gram = pl.pallas_call(
        functools.partial(kernel, nx),
        out_shape=(
            jax.ShapeDtypeStruct((2, PAIRS, 8, 128), F32),
            jax.ShapeDtypeStruct((gr, 128), F32),
        ),
        in_specs=[
            pl.BlockSpec(memory_space=pltpu.HBM),
            pl.BlockSpec(memory_space=pltpu.HBM),
            pl.BlockSpec(memory_space=pltpu.HBM),
        ],
        out_specs=(pl.BlockSpec(memory_space=pltpu.VMEM), pl.BlockSpec(memory_space=pltpu.VMEM)),
        scratch_shapes=scratch,
        compiler_params=pltpu.CompilerParams(
            collective_id=0, has_side_effects=True, vmem_limit_bytes=62 * 1024 * 1024
        ),
    )(design.reshape(2 * half, 128, 128), row_signs.reshape(2 * half, 128), sampled)
    return sketch.reshape(256, 128), gram


def solution(mesh):
    return jax.shard_map(
        functools.partial(on_device, mesh.shape["col"]),
        mesh=mesh,
        in_specs=(P("row", "col"), P("row"), P("row", None)),
        out_specs=(P("row", "col"), P("row", "col")),
        check_vma=False,
    )
```

```python
import functools

import jax
import jax.numpy as jnp
from jax import lax
from jax.experimental import pallas as pl
from jax.experimental.pallas import tpu as pltpu
from jax.sharding import PartitionSpec as P

MESH = pl.DeviceIdType.MESH
NZ, NY = 8, 4
F32, BF16 = jnp.float32, jnp.bfloat16
CHUNKS = 4
PAIRS = 16
LATE = 2
PARTS = (
    ("z", 2, 1, 1),
    ("y", 2, 0, 2),
    ("z", 2, 0, 1),
    ("y", 2, 1, 2),
    ("z", 2, 0, 1),
    ("z", 2, 1, 1),
    ("y", 2, 0, 2),
    ("y", 2, 1, 2),
)
ORDER = (
    (0, 1, 0, 1), (0, 1, 1, 1), (2, 1, 0, 1), (2, 1, 1, 1), (1, 1, 0, 1), (1, 1, 1, 1), (4, 1, 0, 1), (4, 1, 1, 1),
    (5, 1, 0, 1), (5, 1, 1, 1), (3, 1, 0, 1), (3, 1, 1, 1), (0, 1, 0, 2), (0, 1, 1, 2), (2, 1, 0, 2), (2, 1, 1, 2),
    (6, 1, 0, 1), (6, 1, 1, 1), (4, 1, 0, 2), (4, 1, 1, 2), (5, 1, 0, 2), (5, 1, 1, 2), (7, 1, 0, 1), (7, 1, 1, 1),
    (0, 1, 0, 3), (0, 1, 1, 3), (2, 1, 0, 3), (2, 1, 1, 3), (1, 1, 0, 2), (3, 1, 1, 2), (4, 1, 0, 3), (4, 1, 1, 3),
    (5, 1, 0, 3), (5, 1, 1, 3), (6, 1, 0, 2), (7, 1, 1, 2), (0, 1, 1, 4), (2, 1, 0, 4), (1, 2, 0, 1), (3, 2, 0, 1),
    (5, 1, 1, 4), (4, 1, 0, 4), (0, 2, 0, 1), (2, 2, 0, 1), (6, 2, 0, 1), (7, 2, 0, 1), (1, 2, 0, 2), (3, 2, 0, 2),
    (5, 2, 0, 1), (4, 2, 0, 1), (6, 2, 0, 2), (7, 2, 0, 2),
)


def split(v):
    high = v.astype(BF16)
    return high, (v - high.astype(F32)).astype(BF16)


class Arm:
    def __init__(self, stage, step, reach, slot):
        self.stage, self.step, self.reach, self.slot = stage, step, reach, slot
        self.copies = {}

    def start(self, s):
        if not 1 <= s <= self.reach:
            return
        stage, index = self.stage, self.slot + s - 1
        source = stage.source.at[stage.at(self.step * self.reach)] if s == 1 else stage.recv.at[index - 1]
        self.copies[s] = stage.send(index, source, self.step)

    def take(self, s):
        self.copies[s].wait_recv()
        if s < self.reach:
            stage = self.stage
            here = stage.recv.at[self.slot + s - 1]
            here[...] = here[...] + stage.source[stage.at(self.step * (self.reach - s))]
            self.start(s + 1)


class Stage:
    def __init__(self, me, n, longer, scheme, source, recv, send_sem, recv_sem, device, sent):
        self.me, self.n, self.source, self.recv = me, n, source, recv
        self.send_sem, self.recv_sem, self.device, self.sent = send_sem, recv_sem, device, sent
        self.arms = []
        self.two = scheme == 2 and n == 8
        self.direct = scheme > 0 and not self.two
        if self.two:
            s = self.side = -1 if longer else 1
            self.copies = [
                self.send(0, source.at[self.at(-s)], -s),
                self.send(1, source.at[self.at(s)], s),
                self.send(2, source.at[self.at(-3 * s)], -s),
                self.send(3, source.at[self.at(-4 * s)], -2 * s),
                self.send(4, source.at[self.at(3 * s)], s),
            ]
            self.left, self.last = 2, [0, 1, 5, 6]
        elif self.direct:
            self.copies = [self.send(k - 1, source.at[self.at(k)], k) for k in range(1, n)]
            self.left, self.last = 1, list(range(n - 1))
        else:
            long, short = n // 2, n - 1 - n // 2
            up, down = (short, long) if longer else (long, short)
            for step, reach, slot in ((1, up, 0), (-1, down, up)):
                self.arms.append(Arm(self, step, reach, slot))
                self.arms[-1].start(1)
            self.left = n - 1
            self.last = [arm.slot + arm.reach - 1 for arm in self.arms if arm.reach]

    def at(self, offset):
        return lax.rem(self.me + self.n + offset, self.n)

    def send(self, slot, source, offset):
        copy = pltpu.make_async_remote_copy(
            src_ref=source,
            dst_ref=self.recv.at[slot],
            send_sem=self.send_sem.at[slot],
            recv_sem=self.recv_sem.at[slot],
            device_id=self.device(self.at(offset)),
            device_id_type=MESH,
        )
        copy.start()
        self.sent.append(copy)
        return copy

    def take(self, direction, step):
        if self.two and step == 1:
            for slot in (2, 3, 4):
                self.copies[slot].wait_recv()
            s = self.side
            self.recv[2] = self.recv[2] + self.recv[3] + self.source[self.at(-2 * s)]
            self.recv[4] = self.recv[4] + self.source[self.at(2 * s)]
            self.copies += [self.send(5, self.recv.at[2], -2 * s), self.send(6, self.recv.at[4], 2 * s)]
        elif self.two:
            for slot in self.last:
                self.copies[slot].wait_recv()
        elif self.direct:
            if step > 1:
                return False
            for copy in self.copies:
                copy.wait_recv()
        elif step <= self.arms[direction].reach:
            self.arms[direction].take(step)
        else:
            return False
        self.left -= 1
        return self.left == 0

    def total(self):
        value = self.source[self.me]
        for slot in self.last:
            value = value + self.recv[slot]
        return value


def kernel(
    nx, x_hbm, sgn_hbm, smp_hbm, sk_out, g_out,
    x_v, sgn_ref, smp_ref, own, out_t, in_t, sloc, sidx, table, signs0, signs1, sk, beside_sk, packed, xg, gbuf, g2,
    load_sem, t_send, t_recv, i_send, i_recv, x_send, x_recv, h_send, h_recv, *part_refs,
):
    row, col = lax.axis_index("row"), lax.axis_index("col")
    c = lax.rem(row, 2)
    chip = row // 2
    y = lax.rem(chip, NY)
    z = chip // NY
    chips = NZ * NY
    half = PAIRS * 2
    sent = []

    rows_all = 2 * chips
    other = 1 - c

    def at_chip(v):
        return (v * 2 + c, col)

    def at_z(v):
        return at_chip(v * NY + y)

    def at_y(v):
        return at_chip(z * NY + v)

    def other_chip(k):
        return lax.rem(chip + k, chips)

    def other_row(k):
        return lax.rem(row + k, rows_all)

    def other_col(k):
        return lax.rem(col + k, nx)

    beside = row + 1 - 2 * c
    sibling = (beside, col)

    small = []
    for number, (source, target) in enumerate(((smp_hbm, smp_ref), (sgn_hbm, sgn_ref))):
        load = pltpu.make_async_copy(source, target, load_sem.at[2 * CHUNKS + number])
        load.start()
        small.append(load)
    step = half // CHUNKS
    loads = []
    for g in range(CHUNKS):
        for top in range(2):
            rows = pl.ds(top * half + g * step, step)
            load = pltpu.make_async_copy(x_hbm.at[rows], x_v.at[rows], load_sem.at[2 * g + top])
            load.start()
            loads.append(load)

    barrier = pltpu.get_barrier_semaphore()
    for k in range(1, rows_all):
        pl.semaphore_signal(barrier, inc=1, device_id=(other_row(k), col), device_id_type=MESH)
    for k in range(1, nx):
        for there in (row, beside):
            pl.semaphore_signal(barrier, inc=1, device_id=(there, other_col(k)), device_id_type=MESH)

    small[0].wait()
    for h in range(2):
        sloc[h] = smp_ref[:, h * 128 : (h + 1) * 128] & 127
    small[1].wait()

    lane = lax.broadcasted_iota(jnp.int32, (128, 128), 1)
    eye = (lane == lax.broadcasted_iota(jnp.int32, (128, 128), 0)).astype(F32)
    flip = (1 - 2 * c).astype(F32)
    t_copies = []
    for g in range(CHUNKS):
        loads[2 * g].wait()
        loads[2 * g + 1].wait()

        def first(i, _):
            a = g * step + i
            d0 = (eye * sgn_ref[pl.ds(a, 1), :].astype(F32)).astype(BF16)
            d1 = (eye * (sgn_ref[pl.ds(half + a, 1), :].astype(F32) * flip)).astype(BF16)
            v0 = jnp.dot(d0, x_v[a], preferred_element_type=F32)
            v1 = jnp.dot(d1, x_v[half + a], preferred_element_type=F32)
            out_t[a] = v0 - v1
            own[a] = v0 + v1
            return 0

        lax.fori_loop(0, step, first, 0, unroll=4)
        if g == 0:
            pl.semaphore_wait(barrier, rows_all - 1 + 2 * (nx - 1))
        rows = pl.ds(g * step, step)
        copy = pltpu.make_async_remote_copy(
            src_ref=out_t.at[rows],
            dst_ref=in_t.at[rows],
            send_sem=t_send.at[g],
            recv_sem=t_recv.at[g],
            device_id=sibling,
            device_id_type=MESH,
        )
        copy.start()
        t_copies.append(copy)
        if g == 0:
            pltpu.make_async_copy(sloc.at[c], sidx.at[pl.ds(row, 1)], i_recv.at[0]).start()
            for k in range(1, rows_all):
                copy = pltpu.make_async_remote_copy(
                    src_ref=sloc.at[lax.rem(row + k, 2)],
                    dst_ref=sidx.at[pl.ds(row, 1)],
                    send_sem=i_send.at[k - 1],
                    recv_sem=i_recv.at[0],
                    device_id=(other_row(k), col),
                    device_id_type=MESH,
                )
                copy.start()
                sent.append(copy)
    sent += t_copies

    def transform(ref):
        def body(i, _):
            rows = pl.ds(pl.multiple_of(i * 8, 8), 8)
            v = [ref[a, rows, :] for a in range(half)]
            place = 1
            while place < half:
                for a in range(half):
                    if not a & place:
                        v[a], v[a | place] = v[a] + v[a | place], v[a] - v[a | place]
                place *= 2
            for a in range(half):
                ref[a, rows, :] = v[a]
            return 0

        lax.fori_loop(0, 16, body, 0)

    transform(own)

    pltpu.make_async_copy(sidx, sidx, i_recv.at[0]).wait()
    nb = rows_all
    index = sidx[...].astype(F32)
    if nb < 128:
        index = jnp.concatenate([index, jnp.zeros((128 - nb, 128), F32)], axis=0)
    negative = lax.population_count(lane & row) & 1
    table[...] = (index.T.astype(jnp.int32) + 128 * negative).reshape(PAIRS, 8, 128)

    for copy in t_copies:
        copy.wait_recv()
    transform(in_t)

    lower = lax.broadcasted_iota(jnp.int32, (chips * 16, 128), 0) % 8 < 4
    place8 = lax.broadcasted_iota(jnp.int32, (8, 128), 1) + 128
    axes = {"z": (z, NZ, at_z), "y": (y, NY, at_y)}
    stages = {}
    firsts = [sum(kind[1] for kind in PARTS[:number]) for number in range(len(PARTS))]
    for number, (axis, pairs, longer, direct) in enumerate(PARTS):
        q, r1, f, r2, s1, v1, s2, v2 = part_refs[8 * number : 8 * number + 8]
        first_pair = firsts[number]
        n1, n2 = (NZ, NY) if axis == "z" else (NY, NZ)

        def one(p, i, signs):
            index = table[p]
            for place in range(chips):
                bz, by = (place // NY, place % NY) if axis == "z" else (place % NZ, place // NZ)
                rows = []
                for bc in range(2):
                    b = (bz * NY + by) * 2 + bc
                    ours = jnp.broadcast_to(index[:, b : b + 1], (8, 128)) & place8
                    rows.append((1 - 2 * (lax.population_count(ours) & 1)).astype(F32))
                here = pl.ds(place * 16, 16)
                signs[here, :128] = jnp.concatenate(rows, axis=0).astype(BF16)
                signs[here, 128:] = jnp.concatenate([rows[0], -rows[1]], axis=0).astype(BF16)
            field = jnp.concatenate(
                [
                    jnp.concatenate([own[2 * p], own[2 * p + 1]], axis=1),
                    jnp.concatenate([in_t[2 * p], in_t[2 * p + 1]], axis=1),
                ],
                axis=0,
            )
            high, low = split(field)
            both = jnp.dot(signs[...], high, preferred_element_type=F32) + jnp.dot(
                signs[...], low, preferred_element_type=F32
            )
            value = jnp.where(lower, both[:, :128], both[:, 128:])
            q[:, :, i] = value.reshape(n1, n2, 2, 8, 128)

        def product(i, _):
            one(first_pair + 2 * i, 2 * i, signs0)
            one(first_pair + 2 * i + 1, 2 * i + 1, signs1)
            return 0

        if pairs > 1:
            lax.fori_loop(0, pairs // 2, product, 0)
        if pairs % 2:
            one(first_pair + pairs - 1, pairs - 1, signs0)
        me, n, device = axes[axis]
        stages[number, 1] = Stage(me, n, longer, 0, q, r1, s1, v1, device, sent)

    scale = float(8192 * nb) ** (-0.5)
    x_copies = []

    def finish(number):
        here = pl.ds(firsts[number], PARTS[number][1])
        sk[:, here] = jnp.swapaxes(stages[number, 2].total() * scale, 0, 1)
        value = sk[:, here]
        for h in range(2):
            lanes = slice(64 * h, 64 * h + 64)
            packed[h, here] = jnp.concatenate([value[0, :, :, lanes], value[1, :, :, lanes]], axis=2)

        def send(slot, source, target, device):
            copy = pltpu.make_async_remote_copy(
                src_ref=source,
                dst_ref=target,
                send_sem=x_send.at[slot, number],
                recv_sem=x_recv.at[slot, number],
                device_id=device,
                device_id_type=MESH,
            )
            copy.start()
            x_copies.append((number, copy))
            sent.append(copy)

        send(0, sk.at[:, here], beside_sk.at[:, here], sibling)
        for k in range(1, nx):
            send(2 * k - 1, packed.at[c, here], xg.at[k, 0, here], (row, other_col(k)))
            send(2 * k, packed.at[other, here], xg.at[k, 1, here], (beside, other_col(k)))

    gr = nx * 128 // nb
    per_x = rows_all // nx
    group = per_x // 2
    dims = (((0,), (0,)), ((), ()))

    def rows_of(get, numbers):
        return jnp.concatenate(
            [get(pl.ds(firsts[number], PARTS[number][1])).reshape(-1, 128) for number in numbers], axis=0
        )

    def gram(numbers, begin):
        for number, copy in x_copies:
            if number in numbers:
                copy.wait_recv()
        near, far = [], []
        for core, ref in enumerate((sk, beside_sk)):
            near.append(
                jnp.concatenate([rows_of(lambda here, bc=bc: ref[bc, here], numbers) for bc in range(2)], axis=1)
            )
        near = split(jnp.concatenate(near, axis=0))
        for k in range(nx):
            if k:
                far = [rows_of(lambda here, core=core: xg[k, core, here], numbers) for core in range(2)]
            else:
                far = [rows_of(lambda here: packed[c, here], numbers)]
                halves = [
                    jnp.concatenate(
                        [rows_of(lambda here, bc=bc: beside_sk[bc, here], numbers)[:, 64 * h : 64 * h + 64] for bc in range(2)],
                        axis=1,
                    )
                    for h in range(2)
                ]
                far.append(jnp.where(c == 0, halves[0], halves[1]))
            far = split(jnp.concatenate(far, axis=0))
            both = (
                lax.dot_general(far[0], near[0], dims, preferred_element_type=F32)
                + lax.dot_general(far[0], near[1], dims, preferred_element_type=F32)
                + lax.dot_general(far[1], near[0], dims, preferred_element_type=F32)
            )
            block = (both[:64, :128] + both[64:, 128:]).reshape(group, gr, 128)
            here = pl.ds(lax.rem(col + nx - k, nx) * group, group)
            gbuf[here] = block if begin else gbuf[here] + block

    done = []
    for number, phase, direction, step in ORDER:
        if not stages[number, phase].take(direction, step):
            continue
        if phase == 2:
            finish(number)
            done.append(number)
            continue
        axis, pairs, longer, direct = PARTS[number]
        q, r1, f, r2, s1, v1, s2, v2 = part_refs[8 * number : 8 * number + 8]
        f[...] = stages[number, 1].total()
        me, n, device = axes["y" if axis == "z" else "z"]
        stages[number, 2] = Stage(me, n, longer, direct, f, r2, s2, v2, device, sent)
    gram(done[:-LATE], True)
    gram(done[-LATE:], False)

    in_half = lax.rem(row, per_x)
    first_block = row // per_x * group + lax.rem(in_half, group)
    here_too = in_half // group == c

    def to_target(k):
        t = lax.rem(first_block + k, chips)
        return pltpu.make_async_remote_copy(
            src_ref=gbuf.at[t],
            dst_ref=g2.at[chip],
            send_sem=h_send.at[k],
            recv_sem=h_recv.at[0],
            device_id=(t // group * per_x + c * group + lax.rem(t, group), col),
            device_id_type=MESH,
        )

    blocks = [to_target(k) for k in range(chips)]
    for copy in blocks[1:]:
        copy.start()
    pl.when(jnp.logical_not(here_too))(blocks[0].start)

    own_block = pltpu.make_async_copy(gbuf.at[first_block], g2.at[chip], h_recv.at[0])
    pl.when(here_too)(own_block.start)

    sk_out[c] = sk[c]
    sk_out[other] = beside_sk[c]
    for copy in sent:
        copy.wait_send()
    for copy in blocks[1:]:
        copy.wait_send()
    pl.when(jnp.logical_not(here_too))(blocks[0].wait_send)
    pltpu.make_async_copy(g2, g2, h_recv.at[0]).wait()
    g_out[...] = jnp.sum(g2[...], axis=0) * (1.0 / float(256 * nb))


def on_device(nx, design, row_signs, sampled):
    vm, dma = pltpu.VMEM, pltpu.SemaphoreType.DMA
    half = PAIRS * 2
    chips = NZ * NY
    gr = nx * 128 // (2 * chips)
    scratch = [
        vm((2 * half, 128, 128), BF16),
        vm((2 * half, 128), jnp.int32),
        vm((1, 256), jnp.int32),
        vm((half, 128, 128), F32),
        vm((half, 128, 128), F32),
        vm((half, 128, 128), F32),
        vm((2, 1, 128), jnp.int32),
        vm((2 * chips, 128), jnp.int32),
        vm((PAIRS, 8, 128), jnp.int32),
        vm((chips * 16, 256), BF16),
        vm((chips * 16, 256), BF16),
        vm((2, PAIRS, 8, 128), F32),
        vm((2, PAIRS, 8, 128), F32),
        vm((2, PAIRS, 8, 128), F32),
        vm((nx, 2, PAIRS, 8, 128), F32),
        vm((chips, gr, 128), F32),
        vm((chips, gr, 128), F32),
        dma((2 * CHUNKS + 2,)),
        dma((CHUNKS,)),
        dma((CHUNKS,)),
        dma((2 * chips - 1,)),
        dma((1,)),
        dma((2 * nx - 1, len(PARTS))),
        dma((2 * nx - 1, len(PARTS))),
        dma((chips,)),
        dma((1,)),
    ]
    for axis, pairs, _, _ in PARTS:
        n1, n2 = (NZ, NY) if axis == "z" else (NY, NZ)
        scratch += [
            vm((n1, n2, pairs, 2, 8, 128), F32),
            vm((n1 - 1, n2, pairs, 2, 8, 128), F32),
            vm((n2, pairs, 2, 8, 128), F32),
            vm((n2 - 1, pairs, 2, 8, 128), F32),
            dma((n1 - 1,)),
            dma((n1 - 1,)),
            dma((n2 - 1,)),
            dma((n2 - 1,)),
        ]
    sketch, gram = pl.pallas_call(
        functools.partial(kernel, nx),
        out_shape=(
            jax.ShapeDtypeStruct((2, PAIRS, 8, 128), F32),
            jax.ShapeDtypeStruct((gr, 128), F32),
        ),
        in_specs=[
            pl.BlockSpec(memory_space=pltpu.HBM),
            pl.BlockSpec(memory_space=pltpu.HBM),
            pl.BlockSpec(memory_space=pltpu.HBM),
        ],
        out_specs=(pl.BlockSpec(memory_space=pltpu.VMEM), pl.BlockSpec(memory_space=pltpu.VMEM)),
        scratch_shapes=scratch,
        compiler_params=pltpu.CompilerParams(
            collective_id=0, has_side_effects=True, vmem_limit_bytes=48 * 1024 * 1024
        ),
    )(
        *(
            pltpu.with_memory_space_constraint(value, pltpu.HBM)
            for value in (design.reshape(2 * half, 128, 128), row_signs.reshape(2 * half, 128), sampled)
        )
    )
    return sketch.reshape(256, 128), gram


def solution(mesh):
    return jax.shard_map(
        functools.partial(on_device, mesh.shape["col"]),
        mesh=mesh,
        in_specs=(P("row", "col"), P("row"), P("row", None)),
        out_specs=(P("row", "col"), P("row", "col")),
        check_vma=False,
    )
```

```python
import functools

import jax
import jax.numpy as jnp
from jax import lax
from jax.experimental import pallas as pl
from jax.experimental.pallas import tpu as pltpu
from jax.sharding import PartitionSpec as P

MESH = pl.DeviceIdType.MESH
NZ, NY = 8, 4
F32, BF16 = jnp.float32, jnp.bfloat16
CHUNKS = 4
PAIRS = 16
LATE = 2
PARTS = (
    ("z", 2, 1, 1),
    ("y", 2, 0, 2),
    ("z", 2, 0, 1),
    ("y", 2, 1, 2),
    ("z", 2, 0, 1),
    ("z", 2, 1, 1),
    ("y", 2, 0, 2),
    ("y", 2, 1, 2),
)
ORDER = (
    (0, 1, 0, 1), (0, 1, 1, 1), (2, 1, 0, 1), (2, 1, 1, 1), (1, 1, 0, 1), (1, 1, 1, 1), (4, 1, 0, 1), (4, 1, 1, 1),
    (5, 1, 0, 1), (5, 1, 1, 1), (3, 1, 0, 1), (3, 1, 1, 1), (0, 1, 0, 2), (0, 1, 1, 2), (2, 1, 0, 2), (2, 1, 1, 2),
    (6, 1, 0, 1), (6, 1, 1, 1), (4, 1, 0, 2), (4, 1, 1, 2), (5, 1, 0, 2), (5, 1, 1, 2), (7, 1, 0, 1), (7, 1, 1, 1),
    (0, 1, 0, 3), (0, 1, 1, 3), (2, 1, 0, 3), (2, 1, 1, 3), (1, 1, 0, 2), (3, 1, 1, 2), (4, 1, 0, 3), (4, 1, 1, 3),
    (5, 1, 0, 3), (5, 1, 1, 3), (6, 1, 0, 2), (7, 1, 1, 2), (0, 1, 1, 4), (2, 1, 0, 4), (1, 2, 0, 1), (3, 2, 0, 1),
    (5, 1, 1, 4), (4, 1, 0, 4), (0, 2, 0, 1), (2, 2, 0, 1), (6, 2, 0, 1), (7, 2, 0, 1), (1, 2, 0, 2), (3, 2, 0, 2),
    (5, 2, 0, 1), (4, 2, 0, 1), (6, 2, 0, 2), (7, 2, 0, 2),
)


def split(v):
    high = v.astype(BF16)
    return high, (v - high.astype(F32)).astype(BF16)


def arrived(ref, sem):
    pltpu.make_async_copy(ref, ref, sem).wait()


def far_first(n):
    return sorted(range(1, n), key=lambda k: -min(k, n - k))


class Arm:
    def __init__(self, stage, step, reach, slot):
        self.stage, self.step, self.reach, self.slot = stage, step, reach, slot
        self.copies = {}

    def start(self, s):
        if not 1 <= s <= self.reach:
            return
        stage, index = self.stage, self.slot + s - 1
        source = stage.source.at[stage.at(self.step * self.reach)] if s == 1 else stage.recv.at[index - 1]
        self.copies[s] = stage.send(index, source, self.step)

    def take(self, s):
        self.copies[s].wait_recv()
        if s < self.reach:
            stage = self.stage
            here = stage.recv.at[self.slot + s - 1]
            here[...] = here[...] + stage.source[stage.at(self.step * (self.reach - s))]
            self.start(s + 1)


class Stage:
    def __init__(self, me, n, longer, scheme, source, recv, send_sem, recv_sem, device):
        self.me, self.n, self.source, self.recv = me, n, source, recv
        self.send_sem, self.recv_sem, self.device = send_sem, recv_sem, device
        self.arms = []
        self.two = scheme == 2 and n == 8
        self.direct = scheme > 0 and not self.two
        if self.two:
            s = self.side = -1 if longer else 1
            self.send(2, source.at[self.at(-3 * s)], -s)
            self.send(3, source.at[self.at(-4 * s)], -2 * s)
            self.send(4, source.at[self.at(3 * s)], s)
            self.send(0, source.at[self.at(-s)], -s)
            self.send(1, source.at[self.at(s)], s)
            self.left, self.last = 2, [0, 1, 5, 6]
        elif self.direct:
            for k in range(1, n):
                self.send(k - 1, source.at[self.at(k)], k)
            self.left, self.last = 1, list(range(n - 1))
        else:
            long, short = n // 2, n - 1 - n // 2
            up, down = (short, long) if longer else (long, short)
            for step, reach, slot in ((1, up, 0), (-1, down, up)):
                self.arms.append(Arm(self, step, reach, slot))
                self.arms[-1].start(1)
            self.left = n - 1
            self.last = [arm.slot + arm.reach - 1 for arm in self.arms if arm.reach]

    def at(self, offset):
        return lax.rem(self.me + self.n + offset, self.n)

    def send(self, slot, source, offset):
        if self.two:
            arrival = 0 if slot in (2, 3, 4) else 1
        else:
            arrival = 0 if self.direct else slot
        copy = pltpu.make_async_remote_copy(
            src_ref=source,
            dst_ref=self.recv.at[slot],
            send_sem=self.send_sem.at[0],
            recv_sem=self.recv_sem.at[arrival],
            device_id=self.device(self.at(offset)),
            device_id_type=MESH,
        )
        copy.start()
        return copy

    def wait_sends(self):
        arrived(self.recv, self.send_sem.at[0])

    def take(self, direction, step):
        if self.two and step == 1:
            arrived(self.recv.at[pl.ds(2, 3)], self.recv_sem.at[0])
            s = self.side
            self.recv[2] = self.recv[2] + self.recv[3] + self.source[self.at(-2 * s)]
            self.send(5, self.recv.at[2], -2 * s)
            self.recv[4] = self.recv[4] + self.source[self.at(2 * s)]
            self.send(6, self.recv.at[4], 2 * s)
        elif self.two:
            arrived(self.recv.at[pl.ds(0, 4)], self.recv_sem.at[1])
        elif self.direct:
            if step > 1:
                return False
            arrived(self.recv, self.recv_sem.at[0])
        elif step <= self.arms[direction].reach:
            self.arms[direction].take(step)
        else:
            return False
        self.left -= 1
        return self.left == 0

    def total(self):
        value = self.source[self.me]
        for slot in self.last:
            value = value + self.recv[slot]
        return value


def kernel(
    nx, x_hbm, sgn_hbm, smp_hbm, sk_out, g_out,
    x_v, sgn_ref, smp_ref, own, out_t, in_t, sloc, sidx, table, signs0, signs1, sk, beside_sk, packed, xg, gbuf, g2,
    load_sem, t_send, t_recv, i_send, i_recv, x_send, x_recv, h_send, h_recv, *part_refs,
):
    row, col = lax.axis_index("row"), lax.axis_index("col")
    c = lax.rem(row, 2)
    chip = row // 2
    y = lax.rem(chip, NY)
    z = chip // NY
    chips = NZ * NY
    half = PAIRS * 2

    rows_all = 2 * chips
    other = 1 - c

    def at_chip(v):
        return (v * 2 + c, col)

    def at_z(v):
        return at_chip(v * NY + y)

    def at_y(v):
        return at_chip(z * NY + v)

    def other_chip(k):
        return lax.rem(chip + k, chips)

    def other_row(k):
        return lax.rem(row + k, rows_all)

    def other_col(k):
        return lax.rem(col + k, nx)

    beside = row + 1 - 2 * c
    sibling = (beside, col)

    small = []
    for number, (source, target) in enumerate(((smp_hbm, smp_ref), (sgn_hbm, sgn_ref))):
        load = pltpu.make_async_copy(source, target, load_sem.at[CHUNKS + number])
        load.start()
        small.append(load)
    step = half // CHUNKS
    for g in range(CHUNKS):
        for top in range(2):
            rows = pl.ds(top * half + g * step, step)
            load = pltpu.make_async_copy(x_hbm.at[rows], x_v.at[rows], load_sem.at[g])
            load.start()

    barrier = pltpu.get_barrier_semaphore()
    for k in far_first(rows_all):
        pl.semaphore_signal(barrier, inc=1, device_id=(other_row(k), col), device_id_type=MESH)
    for k in range(1, nx):
        for there in (row, beside):
            pl.semaphore_signal(barrier, inc=1, device_id=(there, other_col(k)), device_id_type=MESH)

    small[0].wait()
    for h in range(2):
        sloc[h] = smp_ref[:, h * 128 : (h + 1) * 128] & 127
    pl.semaphore_wait(barrier, rows_all - 1 + 2 * (nx - 1))
    pltpu.make_async_copy(sloc.at[c], sidx.at[pl.ds(row, 1)], i_recv.at[0]).start()
    for k in far_first(rows_all):
        copy = pltpu.make_async_remote_copy(
            src_ref=sloc.at[lax.rem(row + k, 2)],
            dst_ref=sidx.at[pl.ds(row, 1)],
            send_sem=i_send.at[0],
            recv_sem=i_recv.at[0],
            device_id=(other_row(k), col),
            device_id_type=MESH,
        )
        copy.start()
    small[1].wait()

    lane = lax.broadcasted_iota(jnp.int32, (128, 128), 1)
    eye = (lane == lax.broadcasted_iota(jnp.int32, (128, 128), 0)).astype(F32)
    flip = (1 - 2 * c).astype(F32)
    for g in range(CHUNKS):
        arrived(x_v.at[pl.ds(0, 2 * step)], load_sem.at[g])

        def first(i, _):
            a = g * step + i
            d0 = (eye * sgn_ref[pl.ds(a, 1), :].astype(F32)).astype(BF16)
            d1 = (eye * (sgn_ref[pl.ds(half + a, 1), :].astype(F32) * flip)).astype(BF16)
            v0 = jnp.dot(d0, x_v[a], preferred_element_type=F32)
            v1 = jnp.dot(d1, x_v[half + a], preferred_element_type=F32)
            out_t[a] = v0 - v1
            own[a] = v0 + v1
            return 0

        lax.fori_loop(0, step, first, 0, unroll=4)
        rows = pl.ds(g * step, step)
        copy = pltpu.make_async_remote_copy(
            src_ref=out_t.at[rows],
            dst_ref=in_t.at[rows],
            send_sem=t_send.at[0],
            recv_sem=t_recv.at[0],
            device_id=sibling,
            device_id_type=MESH,
        )
        copy.start()

    def transform(ref):
        def body(i, _):
            rows = pl.ds(pl.multiple_of(i * 8, 8), 8)
            v = [ref[a, rows, :] for a in range(half)]
            place = 1
            while place < half:
                for a in range(half):
                    if not a & place:
                        v[a], v[a | place] = v[a] + v[a | place], v[a] - v[a | place]
                place *= 2
            for a in range(half):
                ref[a, rows, :] = v[a]
            return 0

        lax.fori_loop(0, 16, body, 0)

    transform(own)

    arrived(sidx, i_recv.at[0])
    nb = rows_all
    index = sidx[...].astype(F32)
    if nb < 128:
        index = jnp.concatenate([index, jnp.zeros((128 - nb, 128), F32)], axis=0)
    negative = lax.population_count(lane & row) & 1
    table[...] = (index.T.astype(jnp.int32) + 128 * negative).reshape(PAIRS, 8, 128)

    arrived(in_t, t_recv.at[0])
    transform(in_t)

    lower = lax.broadcasted_iota(jnp.int32, (chips * 16, 128), 0) % 8 < 4
    place8 = lax.broadcasted_iota(jnp.int32, (8, 128), 1) + 128
    axes = {"z": (z, NZ, at_z), "y": (y, NY, at_y)}
    stages = {}
    firsts = [sum(kind[1] for kind in PARTS[:number]) for number in range(len(PARTS))]
    for number, (axis, pairs, longer, direct) in enumerate(PARTS):
        q, r1, f, r2, s1, v1, s2, v2 = part_refs[8 * number : 8 * number + 8]
        first_pair = firsts[number]
        n1, n2 = (NZ, NY) if axis == "z" else (NY, NZ)

        def one(p, i, signs):
            index = table[p]
            for place in range(chips):
                bz, by = (place // NY, place % NY) if axis == "z" else (place % NZ, place // NZ)
                rows = []
                for bc in range(2):
                    b = (bz * NY + by) * 2 + bc
                    ours = jnp.broadcast_to(index[:, b : b + 1], (8, 128)) & place8
                    rows.append((1 - 2 * (lax.population_count(ours) & 1)).astype(F32))
                here = pl.ds(place * 16, 16)
                signs[here, :128] = jnp.concatenate(rows, axis=0).astype(BF16)
                signs[here, 128:] = jnp.concatenate([rows[0], -rows[1]], axis=0).astype(BF16)
            field = jnp.concatenate(
                [
                    jnp.concatenate([own[2 * p], own[2 * p + 1]], axis=1),
                    jnp.concatenate([in_t[2 * p], in_t[2 * p + 1]], axis=1),
                ],
                axis=0,
            )
            high, low = split(field)
            both = jnp.dot(signs[...], high, preferred_element_type=F32) + jnp.dot(
                signs[...], low, preferred_element_type=F32
            )
            value = jnp.where(lower, both[:, :128], both[:, 128:])
            q[:, :, i] = value.reshape(n1, n2, 2, 8, 128)

        def product(i, _):
            one(first_pair + 2 * i, 2 * i, signs0)
            one(first_pair + 2 * i + 1, 2 * i + 1, signs1)
            return 0

        if pairs > 1:
            lax.fori_loop(0, pairs // 2, product, 0)
        if pairs % 2:
            one(first_pair + pairs - 1, pairs - 1, signs0)
        me, n, device = axes[axis]
        stages[number, 1] = Stage(me, n, longer, 0, q, r1, s1, v1, device)

    scale = float(8192 * nb) ** (-0.5)

    def finish(number):
        here = pl.ds(firsts[number], PARTS[number][1])
        sk[:, here] = jnp.swapaxes(stages[number, 2].total() * scale, 0, 1)
        value = sk[:, here]
        for h in range(2):
            lanes = slice(64 * h, 64 * h + 64)
            packed[h, here] = jnp.concatenate([value[0, :, :, lanes], value[1, :, :, lanes]], axis=2)

        def send(source, target, device):
            copy = pltpu.make_async_remote_copy(
                src_ref=source,
                dst_ref=target,
                send_sem=x_send.at[number],
                recv_sem=x_recv.at[number],
                device_id=device,
                device_id_type=MESH,
            )
            copy.start()

        for k in far_first(nx):
            send(packed.at[c, here], xg.at[k, 0, here], (row, other_col(k)))
            send(packed.at[other, here], xg.at[k, 1, here], (beside, other_col(k)))
        send(sk.at[:, here], beside_sk.at[:, here], sibling)

    gr = nx * 128 // nb
    per_x = rows_all // nx
    group = per_x // 2
    dims = (((0,), (0,)), ((), ()))

    def x_bytes(number):
        return xg.at[:, :, pl.ds(firsts[number], PARTS[number][1])]

    def rows_of(get, numbers):
        return jnp.concatenate(
            [get(pl.ds(firsts[number], PARTS[number][1])).reshape(-1, 128) for number in numbers], axis=0
        )

    def gram(numbers, begin):
        for number in numbers:
            arrived(x_bytes(number), x_recv.at[number])
        near, far = [], []
        for core, ref in enumerate((sk, beside_sk)):
            near.append(
                jnp.concatenate([rows_of(lambda here, bc=bc: ref[bc, here], numbers) for bc in range(2)], axis=1)
            )
        near = split(jnp.concatenate(near, axis=0))
        for k in range(nx):
            if k:
                far = [rows_of(lambda here, core=core: xg[k, core, here], numbers) for core in range(2)]
            else:
                far = [rows_of(lambda here: packed[c, here], numbers)]
                halves = [
                    jnp.concatenate(
                        [rows_of(lambda here, bc=bc: beside_sk[bc, here], numbers)[:, 64 * h : 64 * h + 64] for bc in range(2)],
                        axis=1,
                    )
                    for h in range(2)
                ]
                far.append(jnp.where(c == 0, halves[0], halves[1]))
            far = split(jnp.concatenate(far, axis=0))
            both = (
                lax.dot_general(far[0], near[0], dims, preferred_element_type=F32)
                + lax.dot_general(far[0], near[1], dims, preferred_element_type=F32)
                + lax.dot_general(far[1], near[0], dims, preferred_element_type=F32)
            )
            block = (both[:64, :128] + both[64:, 128:]).reshape(group, gr, 128)
            here = pl.ds(lax.rem(col + nx - k, nx) * group, group)
            gbuf[here] = block if begin else gbuf[here] + block

    done = []
    for number, phase, direction, step in ORDER:
        if not stages[number, phase].take(direction, step):
            continue
        if phase == 2:
            finish(number)
            done.append(number)
            continue
        axis, pairs, longer, direct = PARTS[number]
        q, r1, f, r2, s1, v1, s2, v2 = part_refs[8 * number : 8 * number + 8]
        f[...] = stages[number, 1].total()
        me, n, device = axes["y" if axis == "z" else "z"]
        stages[number, 2] = Stage(me, n, longer, direct, f, r2, s2, v2, device)
    gram(done[:-LATE], True)
    arrived(sidx.at[pl.ds(0, rows_all - 1)], i_send.at[0])
    arrived(in_t, t_send.at[0])
    for stage in stages.values():
        stage.wait_sends()
    gram(done[-LATE:], False)

    in_half = lax.rem(row, per_x)
    first_block = row // per_x * group + lax.rem(in_half, group)
    here_too = in_half // group == c

    def to_target(k):
        t = lax.rem(first_block + k, chips)
        return pltpu.make_async_remote_copy(
            src_ref=gbuf.at[t],
            dst_ref=g2.at[chip],
            send_sem=h_send.at[0],
            recv_sem=h_recv.at[0],
            device_id=(t // group * per_x + c * group + lax.rem(t, group), col),
            device_id_type=MESH,
        )

    blocks = [to_target(k) for k in range(chips)]
    for k in far_first(chips):
        blocks[k].start()
    pl.when(jnp.logical_not(here_too))(blocks[0].start)

    own_block = pltpu.make_async_copy(gbuf.at[first_block], g2.at[chip], h_recv.at[0])
    pl.when(here_too)(own_block.start)

    sk_out[c] = sk[c]
    sk_out[other] = beside_sk[c]
    for number in range(len(PARTS)):
        arrived(x_bytes(number), x_send.at[number])

    @pl.when(here_too)
    def _():
        arrived(g2.at[pl.ds(0, chips - 1)], h_send.at[0])

    @pl.when(jnp.logical_not(here_too))
    def _():
        arrived(g2, h_send.at[0])

    arrived(g2, h_recv.at[0])
    g_out[...] = jnp.sum(g2[...], axis=0) * (1.0 / float(256 * nb))


def on_device(nx, design, row_signs, sampled):
    vm, dma = pltpu.VMEM, pltpu.SemaphoreType.DMA
    half = PAIRS * 2
    chips = NZ * NY
    gr = nx * 128 // (2 * chips)
    scratch = [
        vm((2 * half, 128, 128), BF16),
        vm((2 * half, 128), jnp.int32),
        vm((1, 256), jnp.int32),
        vm((half, 128, 128), F32),
        vm((half, 128, 128), F32),
        vm((half, 128, 128), F32),
        vm((2, 1, 128), jnp.int32),
        vm((2 * chips, 128), jnp.int32),
        vm((PAIRS, 8, 128), jnp.int32),
        vm((chips * 16, 256), BF16),
        vm((chips * 16, 256), BF16),
        vm((2, PAIRS, 8, 128), F32),
        vm((2, PAIRS, 8, 128), F32),
        vm((2, PAIRS, 8, 128), F32),
        vm((nx, 2, PAIRS, 8, 128), F32),
        vm((chips, gr, 128), F32),
        vm((chips, gr, 128), F32),
        dma((CHUNKS + 2,)),
        dma((1,)),
        dma((1,)),
        dma((1,)),
        dma((1,)),
        dma((len(PARTS),)),
        dma((len(PARTS),)),
        dma((1,)),
        dma((1,)),
    ]
    for axis, pairs, _, scheme in PARTS:
        n1, n2 = (NZ, NY) if axis == "z" else (NY, NZ)
        scratch += [
            vm((n1, n2, pairs, 2, 8, 128), F32),
            vm((n1 - 1, n2, pairs, 2, 8, 128), F32),
            vm((n2, pairs, 2, 8, 128), F32),
            vm((n2 - 1, pairs, 2, 8, 128), F32),
            dma((1,)),
            dma((n1 - 1,)),
            dma((1,)),
            dma((2 if scheme else n2 - 1,)),
        ]
    sketch, gram = pl.pallas_call(
        functools.partial(kernel, nx),
        out_shape=(
            jax.ShapeDtypeStruct((2, PAIRS, 8, 128), F32),
            jax.ShapeDtypeStruct((gr, 128), F32),
        ),
        in_specs=[
            pl.BlockSpec(memory_space=pltpu.HBM),
            pl.BlockSpec(memory_space=pltpu.HBM),
            pl.BlockSpec(memory_space=pltpu.HBM),
        ],
        out_specs=(pl.BlockSpec(memory_space=pltpu.VMEM), pl.BlockSpec(memory_space=pltpu.VMEM)),
        scratch_shapes=scratch,
        compiler_params=pltpu.CompilerParams(
            collective_id=0, has_side_effects=True, vmem_limit_bytes=48 * 1024 * 1024
        ),
    )(
        *(
            pltpu.with_memory_space_constraint(value, pltpu.HBM)
            for value in (design.reshape(2 * half, 128, 128), row_signs.reshape(2 * half, 128), sampled)
        )
    )
    return sketch.reshape(256, 128), gram


def solution(mesh):
    return jax.shard_map(
        functools.partial(on_device, mesh.shape["col"]),
        mesh=mesh,
        in_specs=(P("row", "col"), P("row"), P("row", None)),
        out_specs=(P("row", "col"), P("row", "col")),
        check_vma=False,
    )
```

```python
import functools

import jax
import jax.numpy as jnp
from jax import lax
from jax.experimental import pallas as pl
from jax.experimental.pallas import tpu as pltpu
from jax.sharding import PartitionSpec as P

MESH = pl.DeviceIdType.MESH
NZ, NY = 8, 4
F32, BF16 = jnp.float32, jnp.bfloat16
CHUNKS = 4
PAIRS = 16
LATE = 2
PARTS = (
    ("z", 2, 0, 1),
    ("z", 2, 1, 1),
    ("y", 2, 0, 2),
    ("y", 2, 1, 2),
    ("z", 2, 0, 1),
    ("z", 2, 1, 1),
    ("y", 2, 0, 2),
    ("y", 2, 1, 2),
)
ORDER = (
    (0, 1, 0, 1), (0, 1, 1, 1), (1, 1, 0, 1), (1, 1, 1, 1), (2, 1, 0, 1), (2, 1, 1, 1), (4, 1, 0, 1), (4, 1, 1, 1),
    (5, 1, 0, 1), (5, 1, 1, 1), (3, 1, 0, 1), (3, 1, 1, 1), (0, 1, 0, 2), (0, 1, 1, 2), (1, 1, 0, 2), (1, 1, 1, 2),
    (6, 1, 0, 1), (6, 1, 1, 1), (4, 1, 0, 2), (4, 1, 1, 2), (5, 1, 0, 2), (5, 1, 1, 2), (7, 1, 0, 1), (7, 1, 1, 1),
    (0, 1, 0, 3), (0, 1, 1, 3), (1, 1, 0, 3), (1, 1, 1, 3), (2, 1, 0, 2), (3, 1, 1, 2), (4, 1, 0, 3), (4, 1, 1, 3),
    (5, 1, 0, 3), (5, 1, 1, 3), (6, 1, 0, 2), (0, 1, 0, 4), (7, 1, 1, 2), (1, 1, 1, 4), (2, 2, 0, 1), (3, 2, 0, 1),
    (4, 1, 0, 4), (5, 1, 1, 4), (0, 2, 0, 1), (1, 2, 0, 1), (6, 2, 0, 1), (7, 2, 0, 1), (2, 2, 0, 2), (3, 2, 0, 2),
    (4, 2, 0, 1), (5, 2, 0, 1), (6, 2, 0, 2), (7, 2, 0, 2),
)


def split(v):
    high = v.astype(BF16)
    return high, (v - high.astype(F32)).astype(BF16)


def arrived(ref, sem):
    pltpu.make_async_copy(ref, ref, sem).wait()


def far_first(n):
    return sorted(range(1, n), key=lambda k: -min(k, n - k))


class Arm:
    def __init__(self, stage, step, reach, slot):
        self.stage, self.step, self.reach, self.slot = stage, step, reach, slot
        self.copies = {}

    def start(self, s):
        if not 1 <= s <= self.reach:
            return
        stage, index = self.stage, self.slot + s - 1
        source = stage.source.at[stage.at(self.step * self.reach)] if s == 1 else stage.recv.at[index - 1]
        self.copies[s] = stage.send(index, source, self.step)

    def take(self, s):
        self.copies[s].wait_recv()
        if s < self.reach:
            stage = self.stage
            here = stage.recv.at[self.slot + s - 1]
            here[...] = here[...] + stage.source[stage.at(self.step * (self.reach - s))]
            self.start(s + 1)


class Stage:
    def __init__(self, me, n, longer, scheme, source, recv, send_sem, recv_sem, device):
        self.me, self.n, self.source, self.recv = me, n, source, recv
        self.send_sem, self.recv_sem, self.device = send_sem, recv_sem, device
        self.arms = []
        self.two = scheme == 2 and n == 8
        self.direct = scheme > 0 and not self.two
        if self.two:
            s = self.side = -1 if longer else 1
            self.send(2, source.at[self.at(-3 * s)], -s)
            self.send(3, source.at[self.at(-4 * s)], -2 * s)
            self.send(4, source.at[self.at(3 * s)], s)
            self.send(0, source.at[self.at(-s)], -s)
            self.send(1, source.at[self.at(s)], s)
            self.left, self.last = 2, [0, 1, 5, 6]
        elif self.direct:
            for k in range(1, n):
                self.send(k - 1, source.at[self.at(k)], k)
            self.left, self.last = 1, list(range(n - 1))
        else:
            long, short = n // 2, n - 1 - n // 2
            up, down = (short, long) if longer else (long, short)
            for step, reach, slot in ((1, up, 0), (-1, down, up)):
                self.arms.append(Arm(self, step, reach, slot))
                self.arms[-1].start(1)
            self.left = n - 1
            self.last = [arm.slot + arm.reach - 1 for arm in self.arms if arm.reach]

    def at(self, offset):
        return lax.rem(self.me + self.n + offset, self.n)

    def send(self, slot, source, offset):
        if self.two:
            arrival = 0 if slot in (2, 3, 4) else 1
        else:
            arrival = 0 if self.direct else slot
        copy = pltpu.make_async_remote_copy(
            src_ref=source,
            dst_ref=self.recv.at[slot],
            send_sem=self.send_sem.at[0],
            recv_sem=self.recv_sem.at[arrival],
            device_id=self.device(self.at(offset)),
            device_id_type=MESH,
        )
        copy.start()
        return copy

    def wait_sends(self):
        arrived(self.recv, self.send_sem.at[0])

    def take(self, direction, step):
        if self.two and step == 1:
            arrived(self.recv.at[pl.ds(2, 3)], self.recv_sem.at[0])
            s = self.side
            self.recv[2] = self.recv[2] + self.recv[3] + self.source[self.at(-2 * s)]
            self.send(5, self.recv.at[2], -2 * s)
            self.recv[4] = self.recv[4] + self.source[self.at(2 * s)]
            self.send(6, self.recv.at[4], 2 * s)
        elif self.two:
            arrived(self.recv.at[pl.ds(0, 4)], self.recv_sem.at[1])
        elif self.direct:
            if step > 1:
                return False
            arrived(self.recv, self.recv_sem.at[0])
        elif step <= self.arms[direction].reach:
            self.arms[direction].take(step)
        else:
            return False
        self.left -= 1
        return self.left == 0

    def total(self):
        value = self.source[self.me]
        for slot in self.last:
            value = value + self.recv[slot]
        return value


def kernel(
    nx, x_hbm, sgn_hbm, smp_hbm, sk_out, g_out,
    x_v, sgn_ref, smp_ref, own, out_t, in_t, sloc, sidx, table, signs0, signs1, high, low, sk, beside_sk, packed, xg, gbuf, g2,
    load_sem, t_send, t_recv, i_send, i_recv, x_send, x_recv, h_send, h_recv, *part_refs,
):
    row, col = lax.axis_index("row"), lax.axis_index("col")
    c = lax.rem(row, 2)
    chip = row // 2
    y = lax.rem(chip, NY)
    z = chip // NY
    chips = NZ * NY
    half = PAIRS * 2

    rows_all = 2 * chips
    other = 1 - c

    def at_chip(v):
        return (v * 2 + c, col)

    def at_z(v):
        return at_chip(v * NY + y)

    def at_y(v):
        return at_chip(z * NY + v)

    def other_chip(k):
        return lax.rem(chip + k, chips)

    def other_row(k):
        return lax.rem(row + k, rows_all)

    def other_col(k):
        return lax.rem(col + k, nx)

    beside = row + 1 - 2 * c
    sibling = (beside, col)

    small = []
    for number, (source, target) in enumerate(((smp_hbm, smp_ref), (sgn_hbm, sgn_ref))):
        load = pltpu.make_async_copy(source, target, load_sem.at[CHUNKS + number])
        load.start()
        small.append(load)
    step = half // CHUNKS
    for g in range(CHUNKS):
        for top in range(2):
            rows = pl.ds(top * half + g * step, step)
            load = pltpu.make_async_copy(x_hbm.at[rows], x_v.at[rows], load_sem.at[g])
            load.start()

    barrier = pltpu.get_barrier_semaphore()
    for k in far_first(rows_all):
        pl.semaphore_signal(barrier, inc=1, device_id=(other_row(k), col), device_id_type=MESH)
    for k in range(1, nx):
        for there in (row, beside):
            pl.semaphore_signal(barrier, inc=1, device_id=(there, other_col(k)), device_id_type=MESH)

    small[0].wait()
    for h in range(2):
        sloc[h] = smp_ref[:, h * 128 : (h + 1) * 128] & 127
    pl.semaphore_wait(barrier, rows_all - 1 + 2 * (nx - 1))
    pltpu.make_async_copy(sloc.at[c], sidx.at[pl.ds(row, 1)], i_recv.at[0]).start()
    for k in far_first(rows_all):
        copy = pltpu.make_async_remote_copy(
            src_ref=sloc.at[lax.rem(row + k, 2)],
            dst_ref=sidx.at[pl.ds(row, 1)],
            send_sem=i_send.at[0],
            recv_sem=i_recv.at[0],
            device_id=(other_row(k), col),
            device_id_type=MESH,
        )
        copy.start()
    small[1].wait()

    lane = lax.broadcasted_iota(jnp.int32, (128, 128), 1)
    eye = (lane == lax.broadcasted_iota(jnp.int32, (128, 128), 0)).astype(F32)
    flip = (1 - 2 * c).astype(F32)
    for g in range(CHUNKS):
        arrived(x_v.at[pl.ds(0, 2 * step)], load_sem.at[g])

        def first(i, _):
            a = g * step + i
            d0 = (eye * sgn_ref[pl.ds(a, 1), :].astype(F32)).astype(BF16)
            d1 = (eye * (sgn_ref[pl.ds(half + a, 1), :].astype(F32) * flip)).astype(BF16)
            v0 = jnp.dot(d0, x_v[a], preferred_element_type=F32)
            v1 = jnp.dot(d1, x_v[half + a], preferred_element_type=F32)
            out_t[a] = v0 - v1
            own[a] = v0 + v1
            return 0

        lax.fori_loop(0, step, first, 0, unroll=4)
        rows = pl.ds(g * step, step)
        copy = pltpu.make_async_remote_copy(
            src_ref=out_t.at[rows],
            dst_ref=in_t.at[rows],
            send_sem=t_send.at[0],
            recv_sem=t_recv.at[0],
            device_id=sibling,
            device_id_type=MESH,
        )
        copy.start()

    def transform(ref):
        def body(i, _):
            rows = pl.ds(pl.multiple_of(i * 8, 8), 8)
            v = [ref[a, rows, :] for a in range(half)]
            place = 1
            while place < half:
                for a in range(half):
                    if not a & place:
                        v[a], v[a | place] = v[a] + v[a | place], v[a] - v[a | place]
                place *= 2
            for a in range(half):
                ref[a, rows, :] = v[a]
            return 0

        lax.fori_loop(0, 16, body, 0)

    transform(own)
    arrived(in_t, t_recv.at[0])
    transform(in_t)

    def halve(p, _):
        field = jnp.concatenate(
            [
                jnp.concatenate([own[2 * p], own[2 * p + 1]], axis=1),
                jnp.concatenate([in_t[2 * p], in_t[2 * p + 1]], axis=1),
            ],
            axis=0,
        )
        high[p], low[p] = split(field)
        return 0

    lax.fori_loop(0, PAIRS, halve, 0)

    arrived(sidx, i_recv.at[0])
    nb = rows_all
    index = sidx[...].astype(F32)
    if nb < 128:
        index = jnp.concatenate([index, jnp.zeros((128 - nb, 128), F32)], axis=0)
    negative = lax.population_count(lane & row) & 1
    table[...] = (index.T.astype(jnp.int32) + 128 * negative).reshape(PAIRS, 8, 128)

    lower = lax.broadcasted_iota(jnp.int32, (chips * 16, 128), 0) % 8 < 4
    place8 = lax.broadcasted_iota(jnp.int32, (8, 128), 1) + 128
    axes = {"z": (z, NZ, at_z), "y": (y, NY, at_y)}
    stages = {}
    firsts = [sum(kind[1] for kind in PARTS[:number]) for number in range(len(PARTS))]
    for number, (axis, pairs, longer, direct) in enumerate(PARTS):
        q, r1, f, r2, s1, v1, s2, v2 = part_refs[8 * number : 8 * number + 8]
        first_pair = firsts[number]
        n1, n2 = (NZ, NY) if axis == "z" else (NY, NZ)

        def one(p, i, signs):
            index = table[p]
            for place in range(chips):
                bz, by = (place // NY, place % NY) if axis == "z" else (place % NZ, place // NZ)
                rows = []
                for bc in range(2):
                    b = (bz * NY + by) * 2 + bc
                    ours = jnp.broadcast_to(index[:, b : b + 1], (8, 128)) & place8
                    rows.append((1 - 2 * (lax.population_count(ours) & 1)).astype(F32))
                here = pl.ds(place * 16, 16)
                signs[here, :128] = jnp.concatenate(rows, axis=0).astype(BF16)
                signs[here, 128:] = jnp.concatenate([rows[0], -rows[1]], axis=0).astype(BF16)
            both = jnp.dot(signs[...], high[p], preferred_element_type=F32) + jnp.dot(
                signs[...], low[p], preferred_element_type=F32
            )
            value = jnp.where(lower, both[:, :128], both[:, 128:])
            q[:, :, i] = value.reshape(n1, n2, 2, 8, 128)

        def product(i, _):
            one(first_pair + 2 * i, 2 * i, signs0)
            one(first_pair + 2 * i + 1, 2 * i + 1, signs1)
            return 0

        if pairs > 1:
            lax.fori_loop(0, pairs // 2, product, 0)
        if pairs % 2:
            one(first_pair + pairs - 1, pairs - 1, signs0)
        me, n, device = axes[axis]
        stages[number, 1] = Stage(me, n, longer, 0, q, r1, s1, v1, device)

    scale = float(8192 * nb) ** (-0.5)

    def finish(number):
        here = pl.ds(firsts[number], PARTS[number][1])
        sk[:, here] = jnp.swapaxes(stages[number, 2].total() * scale, 0, 1)
        value = sk[:, here]
        for h in range(2):
            lanes = slice(64 * h, 64 * h + 64)
            packed[h, here] = jnp.concatenate([value[0, :, :, lanes], value[1, :, :, lanes]], axis=2)

        def send(source, target, device):
            copy = pltpu.make_async_remote_copy(
                src_ref=source,
                dst_ref=target,
                send_sem=x_send.at[number],
                recv_sem=x_recv.at[number],
                device_id=device,
                device_id_type=MESH,
            )
            copy.start()

        for k in far_first(nx):
            send(packed.at[c, here], xg.at[k, 0, here], (row, other_col(k)))
            send(packed.at[other, here], xg.at[k, 1, here], (beside, other_col(k)))
        send(sk.at[:, here], beside_sk.at[:, here], sibling)

    gr = nx * 128 // nb
    per_x = rows_all // nx
    group = per_x // 2
    dims = (((0,), (0,)), ((), ()))

    def x_bytes(number):
        return xg.at[:, :, pl.ds(firsts[number], PARTS[number][1])]

    def rows_of(get, numbers):
        return jnp.concatenate(
            [get(pl.ds(firsts[number], PARTS[number][1])).reshape(-1, 128) for number in numbers], axis=0
        )

    def gram(numbers, begin):
        for number in numbers:
            arrived(x_bytes(number), x_recv.at[number])
        near, far = [], []
        for core, ref in enumerate((sk, beside_sk)):
            near.append(
                jnp.concatenate([rows_of(lambda here, bc=bc: ref[bc, here], numbers) for bc in range(2)], axis=1)
            )
        near = split(jnp.concatenate(near, axis=0))
        for k in range(nx):
            if k:
                far = [rows_of(lambda here, core=core: xg[k, core, here], numbers) for core in range(2)]
            else:
                far = [rows_of(lambda here: packed[c, here], numbers)]
                halves = [
                    jnp.concatenate(
                        [rows_of(lambda here, bc=bc: beside_sk[bc, here], numbers)[:, 64 * h : 64 * h + 64] for bc in range(2)],
                        axis=1,
                    )
                    for h in range(2)
                ]
                far.append(jnp.where(c == 0, halves[0], halves[1]))
            far = split(jnp.concatenate(far, axis=0))
            both = (
                lax.dot_general(far[0], near[0], dims, preferred_element_type=F32)
                + lax.dot_general(far[0], near[1], dims, preferred_element_type=F32)
                + lax.dot_general(far[1], near[0], dims, preferred_element_type=F32)
            )
            block = (both[:64, :128] + both[64:, 128:]).reshape(group, gr, 128)
            here = pl.ds(lax.rem(col + nx - k, nx) * group, group)
            gbuf[here] = block if begin else gbuf[here] + block

    done = []
    for number, phase, direction, step in ORDER:
        if not stages[number, phase].take(direction, step):
            continue
        if phase == 2:
            finish(number)
            done.append(number)
            continue
        axis, pairs, longer, direct = PARTS[number]
        q, r1, f, r2, s1, v1, s2, v2 = part_refs[8 * number : 8 * number + 8]
        f[...] = stages[number, 1].total()
        me, n, device = axes["y" if axis == "z" else "z"]
        stages[number, 2] = Stage(me, n, longer, direct, f, r2, s2, v2, device)
    gram(done[:-LATE], True)
    arrived(sidx.at[pl.ds(0, rows_all - 1)], i_send.at[0])
    arrived(in_t, t_send.at[0])
    for stage in stages.values():
        stage.wait_sends()
    gram(done[-LATE:], False)

    in_half = lax.rem(row, per_x)
    first_block = row // per_x * group + lax.rem(in_half, group)
    here_too = in_half // group == c

    def to_target(k):
        t = lax.rem(first_block + k, chips)
        return pltpu.make_async_remote_copy(
            src_ref=gbuf.at[t],
            dst_ref=g2.at[chip],
            send_sem=h_send.at[0],
            recv_sem=h_recv.at[0],
            device_id=(t // group * per_x + c * group + lax.rem(t, group), col),
            device_id_type=MESH,
        )

    blocks = [to_target(k) for k in range(chips)]
    for k in far_first(chips):
        blocks[k].start()
    pl.when(jnp.logical_not(here_too))(blocks[0].start)

    own_block = pltpu.make_async_copy(gbuf.at[first_block], g2.at[chip], h_recv.at[0])
    pl.when(here_too)(own_block.start)

    sk_out[c] = sk[c]
    sk_out[other] = beside_sk[c]
    for number in range(len(PARTS)):
        arrived(x_bytes(number), x_send.at[number])

    @pl.when(here_too)
    def _():
        arrived(g2.at[pl.ds(0, chips - 1)], h_send.at[0])

    @pl.when(jnp.logical_not(here_too))
    def _():
        arrived(g2, h_send.at[0])

    arrived(g2, h_recv.at[0])
    g_out[...] = jnp.sum(g2[...], axis=0) * (1.0 / float(256 * nb))


def on_device(nx, design, row_signs, sampled):
    vm, dma = pltpu.VMEM, pltpu.SemaphoreType.DMA
    half = PAIRS * 2
    chips = NZ * NY
    gr = nx * 128 // (2 * chips)
    scratch = [
        vm((2 * half, 128, 128), BF16),
        vm((2 * half, 128), jnp.int32),
        vm((1, 256), jnp.int32),
        vm((half, 128, 128), F32),
        vm((half, 128, 128), F32),
        vm((half, 128, 128), F32),
        vm((2, 1, 128), jnp.int32),
        vm((2 * chips, 128), jnp.int32),
        vm((PAIRS, 8, 128), jnp.int32),
        vm((chips * 16, 256), BF16),
        vm((chips * 16, 256), BF16),
        vm((PAIRS, 256, 256), BF16),
        vm((PAIRS, 256, 256), BF16),
        vm((2, PAIRS, 8, 128), F32),
        vm((2, PAIRS, 8, 128), F32),
        vm((2, PAIRS, 8, 128), F32),
        vm((nx, 2, PAIRS, 8, 128), F32),
        vm((chips, gr, 128), F32),
        vm((chips, gr, 128), F32),
        dma((CHUNKS + 2,)),
        dma((1,)),
        dma((1,)),
        dma((1,)),
        dma((1,)),
        dma((len(PARTS),)),
        dma((len(PARTS),)),
        dma((1,)),
        dma((1,)),
    ]
    for axis, pairs, _, scheme in PARTS:
        n1, n2 = (NZ, NY) if axis == "z" else (NY, NZ)
        scratch += [
            vm((n1, n2, pairs, 2, 8, 128), F32),
            vm((n1 - 1, n2, pairs, 2, 8, 128), F32),
            vm((n2, pairs, 2, 8, 128), F32),
            vm((n2 - 1, pairs, 2, 8, 128), F32),
            dma((1,)),
            dma((n1 - 1,)),
            dma((1,)),
            dma((2 if scheme else n2 - 1,)),
        ]
    sketch, gram = pl.pallas_call(
        functools.partial(kernel, nx),
        out_shape=(
            jax.ShapeDtypeStruct((2, PAIRS, 8, 128), F32),
            jax.ShapeDtypeStruct((gr, 128), F32),
        ),
        in_specs=[
            pl.BlockSpec(memory_space=pltpu.HBM),
            pl.BlockSpec(memory_space=pltpu.HBM),
            pl.BlockSpec(memory_space=pltpu.HBM),
        ],
        out_specs=(pl.BlockSpec(memory_space=pltpu.VMEM), pl.BlockSpec(memory_space=pltpu.VMEM)),
        scratch_shapes=scratch,
        compiler_params=pltpu.CompilerParams(
            collective_id=0, has_side_effects=True, vmem_limit_bytes=48 * 1024 * 1024
        ),
    )(
        *(
            pltpu.with_memory_space_constraint(value, pltpu.HBM)
            for value in (design.reshape(2 * half, 128, 128), row_signs.reshape(2 * half, 128), sampled)
        )
    )
    return sketch.reshape(256, 128), gram


def solution(mesh):
    return jax.shard_map(
        functools.partial(on_device, mesh.shape["col"]),
        mesh=mesh,
        in_specs=(P("row", "col"), P("row"), P("row", None)),
        out_specs=(P("row", "col"), P("row", "col")),
        check_vma=False,
    )
```

```python
import functools

import jax
import jax.numpy as jnp
from jax import lax
from jax.experimental import pallas as pl
from jax.experimental.pallas import tpu as pltpu
from jax.sharding import PartitionSpec as P

MESH = pl.DeviceIdType.MESH
NZ, NY = 8, 4
F32, BF16 = jnp.float32, jnp.bfloat16
CHUNKS = 4
PAIRS = 16
LATE = 2
PARTS = (
    ("z", 2, 0, 1),
    ("z", 2, 1, 1),
    ("y", 2, 0, 2),
    ("y", 2, 1, 2),
    ("z", 2, 0, 1),
    ("z", 2, 1, 1),
    ("y", 2, 0, 2),
    ("y", 2, 1, 2),
)
ORDER = (
    (0, 1, 0, 1), (0, 1, 1, 1), (1, 1, 0, 1), (1, 1, 1, 1), (2, 1, 0, 1), (2, 1, 1, 1), (4, 1, 0, 1), (4, 1, 1, 1),
    (5, 1, 0, 1), (5, 1, 1, 1), (3, 1, 0, 1), (3, 1, 1, 1), (0, 1, 0, 2), (0, 1, 1, 2), (1, 1, 0, 2), (1, 1, 1, 2),
    (6, 1, 0, 1), (6, 1, 1, 1), (4, 1, 0, 2), (4, 1, 1, 2), (5, 1, 0, 2), (5, 1, 1, 2), (7, 1, 0, 1), (7, 1, 1, 1),
    (0, 1, 0, 3), (0, 1, 1, 3), (1, 1, 0, 3), (1, 1, 1, 3), (2, 1, 0, 2), (3, 1, 1, 2), (4, 1, 0, 3), (4, 1, 1, 3),
    (5, 1, 0, 3), (5, 1, 1, 3), (6, 1, 0, 2), (0, 1, 0, 4), (7, 1, 1, 2), (1, 1, 1, 4), (2, 2, 0, 1), (3, 2, 0, 1),
    (4, 1, 0, 4), (5, 1, 1, 4), (0, 2, 0, 1), (1, 2, 0, 1), (6, 2, 0, 1), (7, 2, 0, 1), (2, 2, 0, 2), (3, 2, 0, 2),
    (4, 2, 0, 1), (5, 2, 0, 1), (6, 2, 0, 2), (7, 2, 0, 2),
)


def split(v):
    high = v.astype(BF16)
    return high, (v - high.astype(F32)).astype(BF16)


def arrived(ref, sem):
    pltpu.make_async_copy(ref, ref, sem).wait()


def far_first(n):
    return sorted(range(1, n), key=lambda k: -min(k, n - k))


class Arm:
    def __init__(self, stage, step, reach, slot):
        self.stage, self.step, self.reach, self.slot = stage, step, reach, slot
        self.copies = {}

    def start(self, s):
        if not 1 <= s <= self.reach:
            return
        stage, index = self.stage, self.slot + s - 1
        source = stage.source.at[stage.at(self.step * self.reach)] if s == 1 else stage.recv.at[index - 1]
        self.copies[s] = stage.send(index, source, self.step)

    def take(self, s):
        self.copies[s].wait_recv()
        if s < self.reach:
            stage = self.stage
            here = stage.recv.at[self.slot + s - 1]
            here[...] = here[...] + stage.source[stage.at(self.step * (self.reach - s))]
            self.start(s + 1)


class Stage:
    def __init__(self, me, n, longer, scheme, source, recv, send_sem, recv_sem, device):
        self.me, self.n, self.source, self.recv = me, n, source, recv
        self.send_sem, self.recv_sem, self.device = send_sem, recv_sem, device
        self.arms = []
        self.two = scheme == 2 and n == 8
        self.direct = scheme > 0 and not self.two
        if self.two:
            s = self.side = -1 if longer else 1
            self.send(2, source.at[self.at(-3 * s)], -s)
            self.send(3, source.at[self.at(-4 * s)], -2 * s)
            self.send(4, source.at[self.at(3 * s)], s)
            self.send(0, source.at[self.at(-s)], -s)
            self.send(1, source.at[self.at(s)], s)
            self.left, self.last = 2, [0, 1, 5, 6]
        elif self.direct:
            for k in range(1, n):
                self.send(k - 1, source.at[self.at(k)], k)
            self.left, self.last = 1, list(range(n - 1))
        else:
            long, short = n // 2, n - 1 - n // 2
            up, down = (short, long) if longer else (long, short)
            for step, reach, slot in ((1, up, 0), (-1, down, up)):
                self.arms.append(Arm(self, step, reach, slot))
                self.arms[-1].start(1)
            self.left = n - 1
            self.last = [arm.slot + arm.reach - 1 for arm in self.arms if arm.reach]

    def at(self, offset):
        return lax.rem(self.me + self.n + offset, self.n)

    def send(self, slot, source, offset):
        if self.two:
            arrival = 0 if slot in (2, 3, 4) else 1
        else:
            arrival = 0 if self.direct else slot
        copy = pltpu.make_async_remote_copy(
            src_ref=source,
            dst_ref=self.recv.at[slot],
            send_sem=self.send_sem.at[0],
            recv_sem=self.recv_sem.at[arrival],
            device_id=self.device(self.at(offset)),
            device_id_type=MESH,
        )
        copy.start()
        return copy

    def wait_sends(self):
        arrived(self.recv, self.send_sem.at[0])

    def take(self, direction, step):
        if self.two and step == 1:
            arrived(self.recv.at[pl.ds(2, 3)], self.recv_sem.at[0])
            s = self.side
            self.recv[2] = self.recv[2] + self.recv[3] + self.source[self.at(-2 * s)]
            self.send(5, self.recv.at[2], -2 * s)
            self.recv[4] = self.recv[4] + self.source[self.at(2 * s)]
            self.send(6, self.recv.at[4], 2 * s)
        elif self.two:
            arrived(self.recv.at[pl.ds(0, 4)], self.recv_sem.at[1])
        elif self.direct:
            if step > 1:
                return False
            arrived(self.recv, self.recv_sem.at[0])
        elif step <= self.arms[direction].reach:
            self.arms[direction].take(step)
        else:
            return False
        self.left -= 1
        return self.left == 0

    def total(self):
        value = self.source[self.me]
        for slot in self.last:
            value = value + self.recv[slot]
        return value


def kernel(
    nx, x_hbm, sgn_hbm, smp_hbm, sk_out, g_out,
    x_v, sgn_ref, smp_ref, own, out_t, in_t, sloc, sidx, table, signs0, signs1, high, low, sk, beside_sk, packed, xg, gbuf, g2,
    load_sem, t_send, t_recv, i_send, i_recv, x_send, x_recv, h_send, h_recv, *part_refs,
):
    row, col = lax.axis_index("row"), lax.axis_index("col")
    c = lax.rem(row, 2)
    chip = row // 2
    y = lax.rem(chip, NY)
    z = chip // NY
    chips = NZ * NY
    half = PAIRS * 2

    rows_all = 2 * chips
    other = 1 - c

    def at_chip(v):
        return (v * 2 + c, col)

    def at_z(v):
        return at_chip(v * NY + y)

    def at_y(v):
        return at_chip(z * NY + v)

    def other_chip(k):
        return lax.rem(chip + k, chips)

    def other_row(k):
        return lax.rem(row + k, rows_all)

    def other_col(k):
        return lax.rem(col + k, nx)

    beside = row + 1 - 2 * c
    sibling = (beside, col)

    small = []
    for number, (source, target) in enumerate(((smp_hbm, smp_ref), (sgn_hbm, sgn_ref))):
        load = pltpu.make_async_copy(source, target, load_sem.at[CHUNKS + number])
        load.start()
        small.append(load)
    step = half // CHUNKS
    for g in range(CHUNKS):
        for top in range(2):
            rows = pl.ds(top * half + g * step, step)
            load = pltpu.make_async_copy(x_hbm.at[rows], x_v.at[rows], load_sem.at[g])
            load.start()

    barrier = pltpu.get_barrier_semaphore()
    for k in far_first(rows_all):
        pl.semaphore_signal(barrier, inc=1, device_id=(other_row(k), col), device_id_type=MESH)
    for k in range(1, nx):
        for there in (row, beside):
            pl.semaphore_signal(barrier, inc=1, device_id=(there, other_col(k)), device_id_type=MESH)

    small[0].wait()
    for h in range(2):
        sloc[h] = smp_ref[:, h * 128 : (h + 1) * 128] & 127
    pl.semaphore_wait(barrier, rows_all - 1 + 2 * (nx - 1))
    pltpu.make_async_copy(sloc.at[c], sidx.at[pl.ds(row, 1)], i_recv.at[0]).start()
    for k in far_first(rows_all):
        copy = pltpu.make_async_remote_copy(
            src_ref=sloc.at[lax.rem(row + k, 2)],
            dst_ref=sidx.at[pl.ds(row, 1)],
            send_sem=i_send.at[0],
            recv_sem=i_recv.at[0],
            device_id=(other_row(k), col),
            device_id_type=MESH,
        )
        copy.start()
    small[1].wait()

    lane = lax.broadcasted_iota(jnp.int32, (128, 128), 1)
    eye = (lane == lax.broadcasted_iota(jnp.int32, (128, 128), 0)).astype(F32)
    flip = (1 - 2 * c).astype(F32)
    for g in range(CHUNKS):
        arrived(x_v.at[pl.ds(0, 2 * step)], load_sem.at[g])

        def first(i, _):
            a = g * step + i
            d0 = (eye * sgn_ref[pl.ds(a, 1), :].astype(F32)).astype(BF16)
            d1 = (eye * (sgn_ref[pl.ds(half + a, 1), :].astype(F32) * flip)).astype(BF16)
            v0 = jnp.dot(d0, x_v[a], preferred_element_type=F32)
            v1 = jnp.dot(d1, x_v[half + a], preferred_element_type=F32)
            out_t[a] = v0 - v1
            own[a] = v0 + v1
            return 0

        lax.fori_loop(0, step, first, 0, unroll=4)
        rows = pl.ds(g * step, step)
        copy = pltpu.make_async_remote_copy(
            src_ref=out_t.at[rows],
            dst_ref=in_t.at[rows],
            send_sem=t_send.at[0],
            recv_sem=t_recv.at[0],
            device_id=sibling,
            device_id_type=MESH,
        )
        copy.start()

    def transform(ref):
        def body(i, _):
            rows = pl.ds(pl.multiple_of(i * 8, 8), 8)
            v = [ref[a, rows, :] for a in range(half)]
            place = 1
            while place < half:
                for a in range(half):
                    if not a & place:
                        v[a], v[a | place] = v[a] + v[a | place], v[a] - v[a | place]
                place *= 2
            for a in range(half):
                ref[a, rows, :] = v[a]
            return 0

        lax.fori_loop(0, 16, body, 0)

    transform(own)
    arrived(in_t, t_recv.at[0])
    transform(in_t)

    def halve(p, _):
        field = jnp.concatenate(
            [
                jnp.concatenate([own[2 * p], own[2 * p + 1]], axis=1),
                jnp.concatenate([in_t[2 * p], in_t[2 * p + 1]], axis=1),
            ],
            axis=0,
        )
        high[p], low[p] = split(field)
        return 0

    lax.fori_loop(0, PAIRS, halve, 0)

    arrived(sidx, i_recv.at[0])
    nb = rows_all
    index = sidx[...].astype(F32)
    if nb < 128:
        index = jnp.concatenate([index, jnp.zeros((128 - nb, 128), F32)], axis=0)
    negative = lax.population_count(lane & row) & 1
    table[...] = (index.T.astype(jnp.int32) + 128 * negative).reshape(PAIRS, 8, 128)

    lower = lax.broadcasted_iota(jnp.int32, (chips * 16, 128), 0) % 8 < 4
    place8 = lax.broadcasted_iota(jnp.int32, (8, 128), 1) + 128
    axes = {"z": (z, NZ, at_z), "y": (y, NY, at_y)}
    stages = {}
    firsts = [sum(kind[1] for kind in PARTS[:number]) for number in range(len(PARTS))]
    for number, (axis, pairs, longer, direct) in enumerate(PARTS):
        q, r1, f, r2, s1, v1, s2, v2 = part_refs[8 * number : 8 * number + 8]
        first_pair = firsts[number]
        n1, n2 = (NZ, NY) if axis == "z" else (NY, NZ)

        def one(p, i, signs):
            index = table[p]
            for place in range(chips):
                bz, by = (place // NY, place % NY) if axis == "z" else (place % NZ, place // NZ)
                rows = []
                for bc in range(2):
                    b = (bz * NY + by) * 2 + bc
                    ours = jnp.broadcast_to(index[:, b : b + 1], (8, 128)) & place8
                    rows.append((1 - 2 * (lax.population_count(ours) & 1)).astype(F32))
                here = pl.ds(place * 16, 16)
                signs[here, :128] = jnp.concatenate(rows, axis=0).astype(BF16)
                signs[here, 128:] = jnp.concatenate([rows[0], -rows[1]], axis=0).astype(BF16)
            both = jnp.dot(signs[...], high[p], preferred_element_type=F32) + jnp.dot(
                signs[...], low[p], preferred_element_type=F32
            )
            value = jnp.where(lower, both[:, :128], both[:, 128:])
            q[:, :, i] = value.reshape(n1, n2, 2, 8, 128)

        def product(i, _):
            one(first_pair + 2 * i, 2 * i, signs0)
            one(first_pair + 2 * i + 1, 2 * i + 1, signs1)
            return 0

        if pairs > 1:
            lax.fori_loop(0, pairs // 2, product, 0)
        if pairs % 2:
            one(first_pair + pairs - 1, pairs - 1, signs0)
        me, n, device = axes[axis]
        stages[number, 1] = Stage(me, n, longer, 0, q, r1, s1, v1, device)

    scale = float(8192 * nb) ** (-0.5)

    def finish(number):
        here = pl.ds(firsts[number], PARTS[number][1])
        sk[:, here] = jnp.swapaxes(stages[number, 2].total() * scale, 0, 1)
        value = sk[:, here]
        for h in range(2):
            lanes = slice(64 * h, 64 * h + 64)
            packed[h, here] = jnp.concatenate([value[0, :, :, lanes], value[1, :, :, lanes]], axis=2)

        def send(source, target, device):
            copy = pltpu.make_async_remote_copy(
                src_ref=source,
                dst_ref=target,
                send_sem=x_send.at[0],
                recv_sem=x_recv.at[0 if len(done) < len(PARTS) - LATE else 1],
                device_id=device,
                device_id_type=MESH,
            )
            copy.start()

        for k in far_first(nx):
            send(packed.at[c, here], xg.at[k, 0, here], (row, other_col(k)))
            send(packed.at[other, here], xg.at[k, 1, here], (beside, other_col(k)))
        send(sk.at[:, here], beside_sk.at[:, here], sibling)

    gr = nx * 128 // nb
    per_x = rows_all // nx
    group = per_x // 2
    dims = (((0,), (0,)), ((), ()))

    def x_bytes(numbers):
        return xg.at[:, :, pl.ds(0, sum(PARTS[number][1] for number in numbers))]

    def rows_of(get, numbers):
        return jnp.concatenate(
            [get(pl.ds(firsts[number], PARTS[number][1])).reshape(-1, 128) for number in numbers], axis=0
        )

    def gram(numbers, begin):
        arrived(x_bytes(numbers), x_recv.at[0 if begin else 1])
        near, far = [], []
        for core, ref in enumerate((sk, beside_sk)):
            near.append(
                jnp.concatenate([rows_of(lambda here, bc=bc: ref[bc, here], numbers) for bc in range(2)], axis=1)
            )
        near = split(jnp.concatenate(near, axis=0))
        for k in range(nx):
            if k:
                far = [rows_of(lambda here, core=core: xg[k, core, here], numbers) for core in range(2)]
            else:
                far = [rows_of(lambda here: packed[c, here], numbers)]
                halves = [
                    jnp.concatenate(
                        [rows_of(lambda here, bc=bc: beside_sk[bc, here], numbers)[:, 64 * h : 64 * h + 64] for bc in range(2)],
                        axis=1,
                    )
                    for h in range(2)
                ]
                far.append(jnp.where(c == 0, halves[0], halves[1]))
            far = split(jnp.concatenate(far, axis=0))
            both = (
                lax.dot_general(far[0], near[0], dims, preferred_element_type=F32)
                + lax.dot_general(far[0], near[1], dims, preferred_element_type=F32)
                + lax.dot_general(far[1], near[0], dims, preferred_element_type=F32)
            )
            block = (both[:64, :128] + both[64:, 128:]).reshape(group, gr, 128)
            here = pl.ds(lax.rem(col + nx - k, nx) * group, group)
            gbuf[here] = block if begin else gbuf[here] + block

    done = []
    for number, phase, direction, step in ORDER:
        if not stages[number, phase].take(direction, step):
            continue
        if phase == 2:
            finish(number)
            done.append(number)
            continue
        axis, pairs, longer, direct = PARTS[number]
        q, r1, f, r2, s1, v1, s2, v2 = part_refs[8 * number : 8 * number + 8]
        f[...] = stages[number, 1].total()
        me, n, device = axes["y" if axis == "z" else "z"]
        stages[number, 2] = Stage(me, n, longer, direct, f, r2, s2, v2, device)
    gram(done[:-LATE], True)
    arrived(sidx.at[pl.ds(0, rows_all - 1)], i_send.at[0])
    arrived(in_t, t_send.at[0])
    for stage in stages.values():
        stage.wait_sends()
    gram(done[-LATE:], False)

    in_half = lax.rem(row, per_x)
    first_block = row // per_x * group + lax.rem(in_half, group)
    here_too = in_half // group == c

    def to_target(k):
        t = lax.rem(first_block + k, chips)
        return pltpu.make_async_remote_copy(
            src_ref=gbuf.at[t],
            dst_ref=g2.at[chip],
            send_sem=h_send.at[0],
            recv_sem=h_recv.at[0],
            device_id=(t // group * per_x + c * group + lax.rem(t, group), col),
            device_id_type=MESH,
        )

    blocks = [to_target(k) for k in range(chips)]
    for k in far_first(chips):
        blocks[k].start()
    pl.when(jnp.logical_not(here_too))(blocks[0].start)

    own_block = pltpu.make_async_copy(gbuf.at[first_block], g2.at[chip], h_recv.at[0])
    pl.when(here_too)(own_block.start)

    sk_out[c] = sk[c]
    sk_out[other] = beside_sk[c]
    arrived(xg, x_send.at[0])

    @pl.when(here_too)
    def _():
        arrived(g2.at[pl.ds(0, chips - 1)], h_send.at[0])

    @pl.when(jnp.logical_not(here_too))
    def _():
        arrived(g2, h_send.at[0])

    arrived(g2, h_recv.at[0])
    g_out[...] = jnp.sum(g2[...], axis=0) * (1.0 / float(256 * nb))


def on_device(nx, design, row_signs, sampled):
    vm, dma = pltpu.VMEM, pltpu.SemaphoreType.DMA
    half = PAIRS * 2
    chips = NZ * NY
    gr = nx * 128 // (2 * chips)
    scratch = [
        vm((2 * half, 128, 128), BF16),
        vm((2 * half, 128), jnp.int32),
        vm((1, 256), jnp.int32),
        vm((half, 128, 128), F32),
        vm((half, 128, 128), F32),
        vm((half, 128, 128), F32),
        vm((2, 1, 128), jnp.int32),
        vm((2 * chips, 128), jnp.int32),
        vm((PAIRS, 8, 128), jnp.int32),
        vm((chips * 16, 256), BF16),
        vm((chips * 16, 256), BF16),
        vm((PAIRS, 256, 256), BF16),
        vm((PAIRS, 256, 256), BF16),
        vm((2, PAIRS, 8, 128), F32),
        vm((2, PAIRS, 8, 128), F32),
        vm((2, PAIRS, 8, 128), F32),
        vm((nx, 2, PAIRS, 8, 128), F32),
        vm((chips, gr, 128), F32),
        vm((chips, gr, 128), F32),
        dma((CHUNKS + 2,)),
        dma((1,)),
        dma((1,)),
        dma((1,)),
        dma((1,)),
        dma((1,)),
        dma((2,)),
        dma((1,)),
        dma((1,)),
    ]
    for axis, pairs, _, scheme in PARTS:
        n1, n2 = (NZ, NY) if axis == "z" else (NY, NZ)
        scratch += [
            vm((n1, n2, pairs, 2, 8, 128), F32),
            vm((n1 - 1, n2, pairs, 2, 8, 128), F32),
            vm((n2, pairs, 2, 8, 128), F32),
            vm((n2 - 1, pairs, 2, 8, 128), F32),
            dma((1,)),
            dma((n1 - 1,)),
            dma((1,)),
            dma(((2 if n2 == 8 and scheme == 2 else 1) if scheme else n2 - 1,)),
        ]
    sketch, gram = pl.pallas_call(
        functools.partial(kernel, nx),
        out_shape=(
            jax.ShapeDtypeStruct((2, PAIRS, 8, 128), F32),
            jax.ShapeDtypeStruct((gr, 128), F32),
        ),
        in_specs=[
            pl.BlockSpec(memory_space=pltpu.HBM),
            pl.BlockSpec(memory_space=pltpu.HBM),
            pl.BlockSpec(memory_space=pltpu.HBM),
        ],
        out_specs=(pl.BlockSpec(memory_space=pltpu.VMEM), pl.BlockSpec(memory_space=pltpu.VMEM)),
        scratch_shapes=scratch,
        compiler_params=pltpu.CompilerParams(
            collective_id=0, has_side_effects=True, vmem_limit_bytes=48 * 1024 * 1024
        ),
    )(
        *(
            pltpu.with_memory_space_constraint(value, pltpu.HBM)
            for value in (design.reshape(2 * half, 128, 128), row_signs.reshape(2 * half, 128), sampled)
        )
    )
    return sketch.reshape(256, 128), gram


def solution(mesh):
    return jax.shard_map(
        functools.partial(on_device, mesh.shape["col"]),
        mesh=mesh,
        in_specs=(P("row", "col"), P("row"), P("row", None)),
        out_specs=(P("row", "col"), P("row", "col")),
        check_vma=False,
    )
```
